128 devices in a mesh: fsdp: 16 (over y_lo, z, core), tp: 8 (over x, y_hi).
Axes of the slice: x: 4, y: 4 (y_hi: 2, y_lo: 2; y = y_hi * 2 + y_lo), z: 4, core: 2. Of those that a mesh axis runs over, the one named last changes fastest.
Arguments:
- hidden_in: bfloat16 [1024, 4096], P('fsdp'), may hold values from -3 to 3
- queries: bfloat16 [2, 1024, 8192], P(None, ('fsdp', 'tp')), may hold values from -170 to 170
- key_cache: bfloat16 [1024, 256, 512], P(('fsdp', 'tp')), may hold values from -6 to 6
- value_cache: bfloat16 [1024, 256, 512], P(('fsdp', 'tp')), may hold values from -6 to 6
- new_keys: bfloat16 [2, 1024, 512], P(None, ('fsdp', 'tp')), may hold values from -6 to 6
- new_values: bfloat16 [2, 1024, 512], P(None, ('fsdp', 'tp')), may hold values from -6 to 6
- lengths: int32 [1024], P(('fsdp', 'tp')), may hold values from 2 to 256
- routes: int32 [2, 1024, 8], P(None, 'fsdp'), may hold values from 0 to 127, all different within a row; in each aligned block of 64 rows (0 to 63, 64 to 127, ..., all dimensions but the last counted through in order) at most 8 rows name the same one
- route_weights: float32 [2, 1024, 8], P(None, 'fsdp'), may hold values from 0.05 to 1
- norm_gain: float32 [4096], replicated, may hold values from 0.1 to 1.9
- gate_master: float32 [8, 1536, 4096], P(None, ('fsdp', 'tp')), may hold values from -0.09375 to 0.09375
- up_master: float32 [8, 1536, 4096], P(None, ('fsdp', 'tp')), may hold values from -0.09375 to 0.09375
- down_master: float32 [8, 1536, 4096], P(None, ('fsdp', 'tp')), may hold values from -0.3125 to 0.3125
- out_proj: bfloat16 [8192, 4096], P('tp'), may hold values from -0.0625 to 0.0625
Outputs:
- hidden_out: bfloat16 [1024, 4096], P('fsdp', 'tp')
- scale_log2: float32 [3, 8, 12, 32], replicated
The draws below stay inside these ranges and needn't reach their ends.
Inputs may be any that keep to these rules, and one draw needn't show every extreme that they name: `routes`: within one step and one index of fsdp (aligned blocks of 64 rows), no expert is named by more than 8 rows.
All inputs are finite; a program needn't handle non-finite values.
Results may differ from the reference program's by a relative error of at most 0.0095.
Values may be sent and summed in bfloat16 or wider, within the bound.
A program may use at most 256 MiB of HBM per device.

```python
import math
import jax
import jax.numpy as jnp
import numpy as np
from jax import lax

D = 4096
FF = 1536
EXPERTS = 128
TOPK = 8
QH = 64
KVH = 4
HD = 128
BLOCK = 128
WIN = 8
STEPS = 2
ROWS = 64
CACHE = 256
TOKENS = 1024
CAP = 8
N_FSDP = 16


def drawn_pair(key):
    cache_keys = jnp.clip(jax.random.normal(jax.random.fold_in(key, 101), (TOKENS, CACHE, KVH * HD), jnp.float32), -6.0, 6.0)
    query_draw = jnp.clip(jax.random.normal(jax.random.fold_in(key, 102), (STEPS, TOKENS, QH * HD), jnp.float32), -6.0, 6.0)
    return (query_draw, cache_keys)


def draw_queries(key, part):
    query_draw, cache_keys = drawn_pair(key)
    return query_draw.astype(jnp.bfloat16)


def draw_key_cache(key, part):
    query_draw, cache_keys = drawn_pair(key)
    return cache_keys.astype(jnp.bfloat16)


def place_ends(entries, rng, low, high):
    extent = entries.shape
    spot = [jax.random.randint(jax.random.fold_in(rng, axis), (), 0, extent[axis]) for axis in range(len(extent))]
    entries = entries.at[tuple(spot)].set(low)
    longest = extent.index(max(extent))
    spot[longest] = (spot[longest] + 1) % extent[longest]
    return entries.at[tuple(spot)].set(high)


def level_of(rng, shape, split, smallest, high):
    loudness, own = 1.0, jax.random.fold_in(rng, 6)
    for dim, parts in split:
        draws = jnp.exp(jax.random.uniform(jax.random.fold_in(own, dim), (parts,), jnp.float32, smallest / len(split), high / len(split)))
        loudness = loudness * jnp.repeat(draws, shape[dim] // parts).reshape([-1 if axis == dim else 1 for axis in range(len(shape))])
    return loudness


def routed_block(own_key, own, number, rows, number_of, top, bound, slope):
    ranking = jax.random.permutation(own_key, number_of)
    heavy_load, ordinary = shares(number_of, rows * top, bound, slope, True), shares(number_of, rows * top, bound, slope, False)
    places = jnp.arange(number_of)

    def named(tallies, offset_by):
        used = int((tallies > 0).sum())
        fixed = max(1, used // 4)
        moved = fixed + (places - fixed + offset_by * (used - fixed)) % max(1, number_of - fixed)
        return jnp.zeros((number_of,), jnp.int32).at[ranking[jnp.where(places < fixed, places, moved)]].set(jnp.asarray(tallies, jnp.int32))

    tallies = jnp.where(number % 4 == 0, named(heavy_load, number // 4), named(ordinary, number - number // 4 - 1))
    mixed = jax.random.permutation(jax.random.fold_in(own, 3), number_of)
    source_of, sink = mixed[0:number_of // 2 * 2:2], mixed[1:number_of // 2 * 2:2]
    slack = jnp.minimum(tallies[source_of] - 1, bound - tallies[sink]) // 2
    slack = jnp.where((source_of == ranking[0]) | (sink == ranking[0]) | (tallies[sink] == 0), 0, jnp.maximum(slack, 0))
    moved = jax.random.randint(jax.random.fold_in(own, 4), (number_of // 2,), 0, 1 << 20) % (slack + 1)
    tallies = tallies.at[source_of].add(-moved).at[sink].add(moved)
    labels = jnp.searchsorted(jnp.cumsum(tallies), jnp.arange(rows * top), side="right").astype(jnp.int32)
    grid = labels.reshape(top, rows).T
    grid = grid[jax.random.permutation(jax.random.fold_in(own, 1), rows)]
    offset_by = jax.random.randint(jax.random.fold_in(own, 2), (rows, 1), 0, top)
    return jnp.take_along_axis(grid, (jnp.arange(top)[None, :] + offset_by) % top, axis=1)


def shares(number_of, total, bound, skew, full):
    weights = [(1 << 20) // math.isqrt(rank ** skew) + 1 for rank in range(1, number_of + 1)]
    largest = bound if full else min(bound, max(-(-total // number_of), total * weights[0] // sum(weights)))
    least = 1 if total - largest >= number_of - 1 else 0
    given, rest = [largest] + [least] * (number_of - 1), total - largest - least * (number_of - 1)
    while rest > 0:
        movable = [i for i in range(1, number_of) if given[i] < largest] or [i for i in range(1, number_of) if given[i] < bound]
        whole, left = sum([weights[i] for i in movable]), rest
        for i in movable:
            addition = min(bound - given[i], max(1, left * weights[i] // whole), rest)
            given[i] = given[i] + addition
            rest = rest - addition
    return np.array(given)


def scatter_about(stream_key, dims, spread, bound, cuts=(), kind=jnp.bfloat16):
    gain = level_of(stream_key, dims, cuts, -0.22, 0.18) if cuts else 1.0
    entries = jax.random.normal(stream_key, dims, jnp.float32) * spread * gain
    return jnp.minimum(jnp.maximum(entries, -bound), bound).astype(kind)


def setup_inputs(seed: int = 0) -> dict:
    streams_of = jax.random.split(jax.random.key(seed), 15)
    hidden_in = scatter_about(streams_of[0], (TOKENS, D), 0.5, 3.0, ((0, 16),))
    queries = draw_queries(jax.random.fold_in(streams_of[14], 71), 0)
    key_cache = draw_key_cache(jax.random.fold_in(streams_of[14], 71), 0)
    value_cache = scatter_about(streams_of[3], (TOKENS, CACHE, KVH * HD), 1.0, 6.0, ((0, 128),))
    new_keys = scatter_about(streams_of[4], (STEPS, TOKENS, KVH * HD), 1.0, 6.0, ((1, 128),))
    new_values = scatter_about(streams_of[5], (STEPS, TOKENS, KVH * HD), 1.0, 6.0, ((1, 128),))
    lengths = place_ends(jax.random.randint(streams_of[6], (TOKENS,), 2, CACHE + 1), jax.random.fold_in(streams_of[6], 1), 2, CACHE).astype(jnp.int32)
    routes_keys = jax.random.split(jax.random.fold_in(streams_of[7], 1), STEPS * TOKENS // ROWS)
    routes_turns = jax.random.permutation(jax.random.fold_in(streams_of[7], 3), STEPS * TOKENS // ROWS)
    routes = jax.vmap(lambda own, number: routed_block(jax.random.fold_in(streams_of[7], 2), own, number, ROWS, EXPERTS, TOPK, CAP, 2))(routes_keys, routes_turns).reshape((STEPS, TOKENS, TOPK))
    route_weights = jnp.clip(jnp.exp(math.log(1.0) - 2.9957323 * jax.random.uniform(streams_of[8], (STEPS, TOKENS, TOPK), jnp.float32) ** level_of(streams_of[8], (STEPS, TOKENS, TOPK), ((1, 16),), -0.2, 0.2)), 0.05, 1.0)
    norm_gain = jnp.clip(1.0 + 0.18 * jax.random.normal(streams_of[9], (D,), jnp.float32), 0.1, 1.9)
    gate_master = scatter_about(streams_of[10], (WIN, FF, D), D ** -0.5, 0.09375, ((1, 128),), jnp.float32)
    up_master = scatter_about(streams_of[11], (WIN, FF, D), D ** -0.5, 0.09375, ((1, 128),), jnp.float32)
    down_master = scatter_about(streams_of[12], (WIN, FF, D), (FF // 4) ** -0.5, 0.3125, ((1, 128),), jnp.float32)
    out_proj = scatter_about(streams_of[13], (QH * HD, D), (QH * HD) ** -0.5, 0.0625, ((0, 8),))
    return dict(hidden_in=hidden_in, queries=queries, key_cache=key_cache, value_cache=value_cache, new_keys=new_keys, new_values=new_values, lengths=lengths, routes=routes, route_weights=route_weights, norm_gain=norm_gain, gate_master=gate_master, up_master=up_master, down_master=down_master, out_proj=out_proj)


neg_fill = -1e+30
epsilon = 1e-06
fp_limit = 448.0
grid_floor = 2.0 ** (-10)
least_exponent = -6.0

def grid_round(values):
    magnitude = jnp.abs(values)
    exponent = jnp.maximum(jnp.floor(jnp.log2(jnp.maximum(magnitude, grid_floor))), least_exponent)
    spacing = jnp.exp2(exponent - 3.0)
    return jnp.sign(values) * jnp.floor(magnitude / spacing + 0.5) * spacing

def quantize(master):
    tiles = master.reshape(WIN, FF // BLOCK, BLOCK, D // BLOCK, BLOCK)
    block_max = lax.optimization_barrier(jnp.max(jnp.abs(tiles), axis=(2, 4)))
    scales = (block_max + epsilon) / fp_limit
    quantized = grid_round(tiles / scales[:, :, None, :, None]).astype(jnp.bfloat16)
    restored = (quantized.astype(jnp.float32) * scales[:, :, None, :, None]).astype(jnp.bfloat16)
    return (restored.reshape(WIN, FF, D), jnp.log2(scales))

def rounded(values):
    return lax.optimization_barrier(values.astype(jnp.bfloat16)).astype(jnp.float32)

def attention_rows(queries_now, cache_keys, cache_values, fresh_keys, fresh_values, lengths):
    row_count = queries_now.shape[0]
    positions = cache_keys.shape[1]
    group = QH // KVH
    score_scale = HD ** (-0.5)
    query_heads = queries_now.astype(jnp.float32).reshape(row_count, KVH, group, HD)
    key_heads = cache_keys.astype(jnp.float32).reshape(row_count, positions, KVH, HD)
    value_heads = cache_values.astype(jnp.float32).reshape(row_count, positions, KVH, HD)
    fresh_count = fresh_keys.shape[1]
    fresh_key_heads = fresh_keys.astype(jnp.float32).reshape(row_count, fresh_count, KVH, HD)
    fresh_value_heads = fresh_values.astype(jnp.float32).reshape(row_count, fresh_count, KVH, HD)
    cached_scores = jnp.einsum('rkgd,rpkd->rkgp', query_heads, key_heads) * score_scale
    fresh_scores = jnp.einsum('rkgd,rskd->rkgs', query_heads, fresh_key_heads) * score_scale
    alive_mask = (jnp.arange(positions, dtype=jnp.int32)[None, :] < lengths[:, None])[:, None, None, :]
    peak_score = jnp.maximum(lax.optimization_barrier(jnp.max(jnp.where(alive_mask, cached_scores, neg_fill), axis=-1)), lax.optimization_barrier(jnp.max(fresh_scores, axis=-1)))
    cached_weights = jnp.where(alive_mask, jnp.exp(cached_scores - peak_score[..., None]), 0.0)
    fresh_weights = jnp.exp(fresh_scores - peak_score[..., None])
    weight_sum = lax.optimization_barrier(jnp.sum(cached_weights, axis=-1)) + lax.optimization_barrier(jnp.sum(fresh_weights, axis=-1))
    cached_probs = rounded(cached_weights / weight_sum[..., None])
    fresh_probs = rounded(fresh_weights / weight_sum[..., None])
    output = jnp.einsum('rkgp,rpkd->rkgd', cached_probs, value_heads) + jnp.einsum('rkgs,rskd->rkgd', fresh_probs, fresh_value_heads)
    return output.astype(jnp.bfloat16).reshape(row_count, QH * HD)

def rms_norm(mixed, norm_gain):
    values = mixed.astype(jnp.float32)
    inverse = lax.rsqrt(lax.optimization_barrier(jnp.mean(values * values, axis=-1, keepdims=True)) + epsilon)
    return (values * inverse * norm_gain[None, :]).astype(jnp.bfloat16)

def routing_tables(routes, route_weights, capacity):
    weight_sum = lax.optimization_barrier(jnp.sum(route_weights, axis=1))
    experts = jnp.arange(WIN, dtype=jnp.int32)
    matches = routes[None, :, :] == experts[:, None, None]
    chosen = jnp.any(matches, axis=2)
    gate_share = lax.optimization_barrier(jnp.sum(jnp.where(matches, route_weights[None, :, :], 0.0), axis=2)) / weight_sum[None, :]
    slot_index = jnp.cumsum(chosen.astype(jnp.int32), axis=1) - 1
    places = jnp.arange(capacity, dtype=jnp.int32)
    picked = (slot_index[:, None, :] == places[None, :, None]) & chosen[:, None, :]
    return (picked.astype(jnp.float32), picked.astype(jnp.float32) * gate_share[:, None, :])

def expert_rows(selected, gate_rows, up_rows, down_rows):
    gate_act = jnp.einsum('ecd,ehd->ech', selected.astype(jnp.float32), gate_rows.astype(jnp.float32))
    up_act = jnp.einsum('ecd,ehd->ech', selected.astype(jnp.float32), up_rows.astype(jnp.float32))
    product = (jax.nn.silu(gate_act) * up_act).astype(jnp.bfloat16)
    return jnp.einsum('ech,ehd->ecd', product.astype(jnp.float32), down_rows.astype(jnp.float32))

def reference(hidden_in, queries, key_cache, value_cache, new_keys, new_values, lengths, routes, route_weights, norm_gain, gate_master, up_master, down_master, out_proj):
    gate_rows, gate_log = quantize(gate_master)
    up_rows, up_log = quantize(up_master)
    down_rows, down_log = quantize(down_master)
    scale_log2 = jnp.stack([gate_log, up_log, down_log])
    block_count = TOKENS // ROWS
    width = KVH * HD
    current = hidden_in
    for step_index in range(STEPS):
        fresh_count = step_index + 1
        fresh_keys = jnp.transpose(new_keys[:fresh_count], (1, 0, 2)).reshape(block_count, ROWS, fresh_count, width)
        fresh_values = jnp.transpose(new_values[:fresh_count], (1, 0, 2)).reshape(block_count, ROWS, fresh_count, width)
        blocked = (queries[step_index].reshape(block_count, ROWS, QH * HD), key_cache.reshape(block_count, ROWS, CACHE, width), value_cache.reshape(block_count, ROWS, CACHE, width), fresh_keys, fresh_values, lengths.reshape(block_count, ROWS))
        heads = lax.map(lambda items: attention_rows(*items), blocked).reshape(TOKENS, QH * HD)
        projected = jnp.dot(heads, out_proj, preferred_element_type=jnp.float32)
        mixed = (current.astype(jnp.float32) + projected).astype(jnp.bfloat16)
        normed = rms_norm(mixed, norm_gain)
        picked, weighted = routing_tables(routes[step_index], route_weights[step_index], CAP * N_FSDP)
        selected = jnp.einsum('ecr,rd->ecd', picked, normed.astype(jnp.float32)).astype(jnp.bfloat16)
        outputs = expert_rows(selected, gate_rows, up_rows, down_rows)
        moe = jnp.einsum('ecr,ecd->rd', weighted, outputs, precision=lax.Precision.HIGHEST)
        current = (mixed.astype(jnp.float32) + moe).astype(jnp.bfloat16)
    return (current, scale_log2)
```

```python
import jax
import jax.numpy as jnp
from jax import lax
from jax.sharding import PartitionSpec as P

D = 4096
FF = 1536
QH = 64
KVH = 4
HD = 128
BLOCK = 128
WIN = 8
CAP = 8


neg_fill = -1e30
epsilon = 1e-06
fp_limit = 448.0
grid_floor = 2.0 ** (-10)
least_exponent = -6.0


def cut_along(array, dim, peers):
    before, after = (array.shape[:dim], array.shape[dim + 1 :])
    return jnp.moveaxis(array.reshape(*before, peers, -1, *after), dim, 0)


def sent_and_summed(array, axis, dim):
    blocks = cut_along(array, dim, lax.axis_size(axis))
    arrived = lax.all_to_all(blocks, axis, split_axis=0, concat_axis=0, tiled=True)
    return arrived.astype(jnp.float32).sum(axis=0)


def copy_for_each(array, axis):
    peers = lax.axis_size(axis)
    return lax.all_to_all(
        jnp.broadcast_to(array[None], (peers, *array.shape)), axis, 0, 0, tiled=True
    )


def joined_along(blocks, dim):
    blocks = jnp.moveaxis(blocks, 0, dim)
    lengths = blocks.shape
    return blocks.reshape(*lengths[:dim], lengths[dim] * lengths[dim + 1], *lengths[dim + 2 :])


def collect(array, axis, dim):
    blocks = copy_for_each(array, axis)
    return joined_along(blocks, dim)


def grid_round(values):
    magnitude = jnp.abs(values)
    exponent = jnp.maximum(jnp.floor(jnp.log2(jnp.maximum(magnitude, grid_floor))), least_exponent)
    spacing = jnp.exp2(exponent - 3.0)
    return jnp.sign(values) * jnp.floor(magnitude / spacing + 0.5) * spacing


def attention_rows(queries_now, cache_keys, cache_values, fresh_keys, fresh_values, lengths):
    row_count = queries_now.shape[0]
    positions = cache_keys.shape[1]
    group = QH // KVH
    score_scale = HD ** (-0.5)
    fresh_count = fresh_keys.shape[0]
    query_heads = queries_now.reshape(row_count, KVH, group, HD)
    key_heads = cache_keys.reshape(row_count, positions, KVH, HD)
    value_heads = cache_values.reshape(row_count, positions, KVH, HD)
    fresh_key_heads = fresh_keys.reshape(fresh_count, row_count, KVH, HD)
    fresh_value_heads = fresh_values.reshape(fresh_count, row_count, KVH, HD)
    cached_scores = (
        jnp.einsum("rkgd,rpkd->rkgp", query_heads, key_heads, preferred_element_type=jnp.float32)
        * score_scale
    )
    fresh_scores = (
        jnp.einsum(
            "rkgd,srkd->rkgs", query_heads, fresh_key_heads, preferred_element_type=jnp.float32
        )
        * score_scale
    )
    alive_mask = (jnp.arange(positions, dtype=jnp.int32)[None, :] < lengths[:, None])[
        :, None, None, :
    ]
    peak_score = jnp.maximum(
        jnp.max(jnp.where(alive_mask, cached_scores, neg_fill), axis=-1),
        jnp.max(fresh_scores, axis=-1),
    )
    cached_weights = jnp.where(alive_mask, jnp.exp(cached_scores - peak_score[..., None]), 0.0)
    fresh_weights = jnp.exp(fresh_scores - peak_score[..., None])
    weight_sum = jnp.sum(cached_weights, axis=-1) + jnp.sum(fresh_weights, axis=-1)
    cached_probs = (cached_weights / weight_sum[..., None]).astype(jnp.bfloat16)
    fresh_probs = (fresh_weights / weight_sum[..., None]).astype(jnp.bfloat16)
    output = jnp.einsum(
        "rkgp,rpkd->rkgd", cached_probs, value_heads, preferred_element_type=jnp.float32
    )
    output = output + jnp.einsum(
        "rkgs,srkd->rkgd", fresh_probs, fresh_value_heads, preferred_element_type=jnp.float32
    )
    return output.astype(jnp.bfloat16).reshape(row_count, QH * HD)


def routing_tables(routes, route_weights):
    rows = routes.shape[0]
    weight_sum = jnp.sum(route_weights, axis=1)
    experts = jnp.arange(WIN, dtype=jnp.int32)
    matches = routes[None, :, :] == experts[:, None, None]
    chosen = jnp.any(matches, axis=2)
    gate_share = (
        jnp.sum(jnp.where(matches, route_weights[None, :, :], 0.0), axis=2) / weight_sum[None, :]
    )
    earlier = jnp.arange(rows)[:, None] < jnp.arange(rows)[None, :]
    slot_index = jnp.sum(jnp.where(earlier[None], chosen.astype(jnp.int32)[:, :, None], 0), axis=1)
    places = jnp.arange(CAP, dtype=jnp.int32)
    picked = (slot_index[:, None, :] == places[None, :, None]) & chosen[:, None, :]
    slot_share = jnp.sum(jnp.where(picked, gate_share[:, None, :], 0.0), axis=2)
    return (picked.astype(jnp.bfloat16), slot_share)


def block_maxima(masters, fsdp_pos, tp_pos, tp_count):
    shard_rows = masters.shape[2]
    magnitude = jnp.max(jnp.abs(masters).reshape(3, WIN, shard_rows, D // BLOCK, BLOCK), axis=4)
    first_tile = (fsdp_pos * shard_rows * tp_count) // BLOCK
    owned = (fsdp_pos * tp_count + tp_pos) * shard_rows + jnp.arange(shard_rows, dtype=jnp.int32)
    second = (owned // BLOCK - first_tile) == 1
    mine = jnp.stack(
        [
            jnp.max(jnp.where(second[None, None, :, None], 0.0, magnitude), axis=2),
            jnp.max(jnp.where(second[None, None, :, None], magnitude, 0.0), axis=2),
        ]
    )
    group = jnp.max(copy_for_each(mine, "tp"), axis=0)
    every = copy_for_each(group, "fsdp")
    tiles = []
    for tile in range(FF // BLOCK):
        parts = []
        for owner in range(16):
            first = owner * 96 // BLOCK
            if first == tile:
                parts.append(every[owner, 0])
            if first + 1 == tile and owner * 96 + 95 >= tile * BLOCK:
                parts.append(every[owner, 1])
        tiles.append(jnp.max(jnp.stack(parts), axis=0))
    return jnp.stack(tiles, axis=2), first_tile, second


def local(
    hidden_in,
    queries,
    key_cache,
    value_cache,
    new_keys,
    new_values,
    lengths,
    routes,
    route_weights,
    norm_gain,
    gate_master,
    up_master,
    down_master,
    out_proj,
):
    tp_count = lax.axis_size("tp")
    fsdp_pos = lax.axis_index("fsdp")
    tp_pos = lax.axis_index("tp")
    shard_rows = gate_master.shape[1]
    masters = jnp.stack([gate_master, up_master, down_master])
    block_max, first_tile, second = block_maxima(masters, fsdp_pos, tp_pos, tp_count)
    scales = (block_max + epsilon) / fp_limit
    scale_log2 = jnp.log2(scales)
    near = lax.dynamic_slice_in_dim(scales, first_tile, 1, 2)
    far = lax.dynamic_slice_in_dim(scales, jnp.minimum(first_tile + 1, FF // BLOCK - 1), 1, 2)
    factors = jnp.where(second[None, None, :, None], far, near)[..., None]
    tiles = masters.reshape(3, WIN, shard_rows, D // BLOCK, BLOCK)
    quantized = grid_round(tiles / factors).astype(jnp.bfloat16).astype(jnp.float32)
    restored = (quantized * factors).astype(jnp.bfloat16).reshape(3, WIN, shard_rows, D)
    arrived = lax.all_to_all(
        restored.transpose(1, 0, 2, 3), "tp", split_axis=0, concat_axis=0, tiled=True
    )
    own = [arrived[:, i].reshape(tp_count * shard_rows, D) for i in range(3)]

    share_cols = D // tp_count
    own_start = tp_pos * share_cols
    current = lax.dynamic_slice_in_dim(hidden_in, own_start, share_cols, 1)
    tables = [routing_tables(routes[s], route_weights[s]) for s in range(2)]
    heads = jnp.stack(
        [
            attention_rows(
                queries[s], key_cache, value_cache, new_keys[: s + 1], new_values[: s + 1], lengths
            )
            for s in range(2)
        ]
    )
    regrouped = lax.all_to_all(heads, "tp", split_axis=2, concat_axis=1, tiled=True)
    projections = []
    for s in range(2):
        projected = jnp.dot(regrouped[s], out_proj, preferred_element_type=jnp.float32)
        projections.append(projected.astype(jnp.bfloat16))
    both = jnp.stack(projections)
    summed = sent_and_summed(both, "tp", 2)
    for s in range(2):
        picked, slot_share = tables[s]
        mixed = (current.astype(jnp.float32) + summed[s]).astype(jnp.bfloat16)
        slots = picked.reshape(WIN * CAP, -1)
        chosen = jnp.dot(slots, mixed, preferred_element_type=jnp.float32).astype(jnp.bfloat16)
        rows = collect_slots(chosen)
        values = rows.astype(jnp.float32)
        inverse = lax.rsqrt(jnp.mean(values * values, axis=1, keepdims=True) + epsilon)
        normed = (values * inverse * norm_gain[None, :]).astype(jnp.bfloat16)
        everyone = copy_for_each(normed, "fsdp").reshape(-1, D)
        gate = jnp.einsum("rd,hd->rh", everyone, own[0], preferred_element_type=jnp.float32)
        up = jnp.einsum("rd,hd->rh", everyone, own[1], preferred_element_type=jnp.float32)
        act = (jax.nn.silu(gate) * up).astype(jnp.bfloat16)
        partial = jnp.dot(act, own[2], preferred_element_type=jnp.float32).astype(jnp.bfloat16)
        output = sent_and_summed(partial, "fsdp", 0)
        share = lax.dynamic_slice_in_dim(slot_share, tp_pos, 1, 0)[0]
        weighted = (output * share[:, None]).astype(jnp.bfloat16)
        returned = lax.all_to_all(
            cut_along(weighted, 1, tp_count), "tp", split_axis=0, concat_axis=0, tiled=True
        ).reshape(WIN * CAP, share_cols)
        moe = lax.dot_general(
            slots, returned, (((0,), (0,)), ((), ())), preferred_element_type=jnp.float32
        )
        current = (mixed.astype(jnp.float32) + moe).astype(jnp.bfloat16)
    return (current, scale_log2)


def collect_slots(chosen):
    arrived = lax.all_to_all(chosen, "tp", split_axis=0, concat_axis=0, tiled=True)
    blocks = arrived.reshape(-1, CAP, chosen.shape[1])
    return joined_along(blocks, 1)


def solution(mesh):
    in_specs = (
        P("fsdp", None),
        P(None, ("fsdp", "tp"), None),
        P(("fsdp", "tp"), None, None),
        P(("fsdp", "tp"), None, None),
        P(None, ("fsdp", "tp"), None),
        P(None, ("fsdp", "tp"), None),
        P(("fsdp", "tp")),
        P(None, "fsdp", None),
        P(None, "fsdp", None),
        P(),
        P(None, ("fsdp", "tp"), None),
        P(None, ("fsdp", "tp"), None),
        P(None, ("fsdp", "tp"), None),
        P("tp", None),
    )
    out_specs = (P("fsdp", "tp"), P())
    return jax.shard_map(local, mesh=mesh, in_specs=in_specs, out_specs=out_specs, check_vma=False)
```

```python
import jax
import jax.numpy as jnp
from jax import lax
from jax.experimental import pallas as pl
from jax.experimental.pallas import tpu as pltpu
from jax.sharding import PartitionSpec as P

D = 4096
FF = 1536
QH = 64
KVH = 4
HD = 128
BLOCK = 128
WIN = 8
CAP = 8
STEPS = 2
ROWS = 64
CACHE = 256
N_FSDP = 16
N_TP = 8
SHARD = FF // (N_FSDP * N_TP)
TILES = FF // BLOCK
COLS = D // BLOCK
SHARE = D // N_TP
QUARTER = D // 4
FOLD = 4 * SHARD

neg_fill = -1e30
epsilon = 1e-06
fp_limit = 448.0
tie_nudge = 1.0 + 2.0**-22

f32 = jnp.float32
bf16 = jnp.bfloat16


def nt_dot(a, b):
    return lax.dot_general(a, b, (((1,), (1,)), ((), ())), preferred_element_type=f32)


def nn_dot(a, b):
    return lax.dot_general(a, b, (((1,), (0,)), ((), ())), preferred_element_type=f32)


def iota(shape, dim):
    return lax.broadcasted_iota(jnp.int32, shape, dim)


def kernel(
    hidden,
    queries,
    key_cache,
    value_cache,
    new_keys,
    new_values,
    lengths,
    routes,
    route_weights,
    gain,
    gate_master,
    up_master,
    down_master,
    out_proj,
    out,
    logs,
    mast,
    qbuf,
    kbuf,
    vbuf,
    wproj,
    cur,
    mine,
    x1r,
    every,
    bm,
    sendw,
    wbuf,
    sendh,
    recvh,
    sendp,
    recvp,
    slots,
    slots_t,
    share,
    mixed,
    sendd,
    recvd,
    sende,
    recve,
    sendg,
    recvg,
    sendr,
    recvr,
    spread,
    local_sem,
    x1s,
    x1q,
    x2s,
    x2q,
    hs,
    hq,
    ws,
    wq,
    cs,
    cq,
    ps,
    pq,
    ds,
    dq,
    es,
    eq,
    gs,
    gq,
    rs,
    rq,
):
    f = lax.axis_index("fsdp")
    t = lax.axis_index("tp")
    k = f // 2
    core = lax.rem(f, 2)
    partner = f + 1 - 2 * core

    def tp_peer(d):
        return lax.rem(t + d, N_TP)

    def chip_peer(d):
        return lax.rem(k + d, 8)

    def remote(src, dst, send, recv, to):
        return pltpu.make_async_remote_copy(
            src_ref=src,
            dst_ref=dst,
            send_sem=send,
            recv_sem=recv,
            device_id=to,
            device_id_type=pl.DeviceIdType.MESH,
        )

    def each(low, high, body):
        def step(d, carry):
            body(d)
            return carry

        lax.fori_loop(low, high, step, 0)

    own_cols = pl.ds(pl.multiple_of(t * SHARE, SHARE), SHARE)
    loads = [
        pltpu.make_async_copy(queries, qbuf, local_sem.at[3]),
        pltpu.make_async_copy(key_cache, kbuf, local_sem.at[4]),
        pltpu.make_async_copy(value_cache, vbuf, local_sem.at[5]),
        pltpu.make_async_copy(hidden.at[:, own_cols], cur, local_sem.at[6]),
        pltpu.make_async_copy(out_proj, wproj, local_sem.at[7]),
    ]
    for m, master in enumerate((gate_master, up_master, down_master)):

        def load_columns(c, m=m, master=master):
            cols = pl.ds(pl.multiple_of(c * BLOCK, BLOCK), BLOCK)
            pltpu.make_async_copy(master.at[:, cols], mast.at[m, c], local_sem.at[m]).start()

        each(0, COLS, load_columns)
    for load in loads:
        load.start()

    barrier = pltpu.get_barrier_semaphore()

    def greet(to):
        pl.semaphore_signal(barrier, inc=1, device_id=to, device_id_type=pl.DeviceIdType.MESH)

    each(1, N_TP, lambda d: greet((f, tp_peer(d))))
    each(1, N_FSDP, lambda d: greet((lax.rem(f + d, N_FSDP), t)))

    lane64 = iota((ROWS, ROWS), 1)
    row64 = iota((ROWS, ROWS), 0)
    earlier = (row64 < lane64).astype(f32).astype(bf16)
    expert_rows = iota((WIN, ROWS), 0)
    for s in range(STEPS):
        names = routes[s]
        weights = route_weights[s]
        total = jnp.sum(weights, axis=0, keepdims=True)
        chosen = jnp.zeros((WIN, ROWS), f32)
        shares = jnp.zeros((WIN, ROWS), f32)
        for e in range(WIN):
            match = names == e
            has = jnp.max(jnp.where(match, 1.0, 0.0), axis=0, keepdims=True)
            sums = jnp.sum(jnp.where(match, weights, 0.0), axis=0, keepdims=True)
            chosen = jnp.where(expert_rows == e, has, chosen)
            shares = jnp.where(expert_rows == e, sums, shares)
        shares = shares / total
        place = nn_dot(chosen.astype(bf16), earlier)
        place = jnp.where(chosen > 0.5, place, 1000.0)
        place_index = iota((WIN, CAP, ROWS), 1).astype(f32)
        picked = jnp.where(place[:, None, :] == place_index, 1.0, 0.0)
        picked2 = picked.reshape(WIN * CAP, ROWS)
        slots[s] = picked2.astype(bf16)
        slots_t[s] = picked2.T.astype(bf16)
        slot_share = jnp.sum(picked * shares[:, None, :], axis=2, keepdims=True)
        share[s] = jnp.broadcast_to(slot_share.reshape(WIN * CAP, 1), (WIN * CAP, BLOCK))
    column = iota((8 * FOLD, 8 * FOLD), 1)
    line = iota((8 * FOLD, 8 * FOLD), 0)
    same = ((column // FOLD) == (line // FOLD)) & (lax.rem(column, SHARD) == lax.rem(line, SHARD))
    spread[...] = jnp.where(same, 1.0, 0.0).astype(bf16)

    first_tile = (f * (N_TP * SHARD)) // BLOCK
    first_row = (f * N_TP + t) * SHARD
    border = (first_tile + 1) * BLOCK - first_row
    lane = iota((WIN, BLOCK), 1)
    zero = jnp.zeros((WIN, BLOCK), f32)
    near_max, far_max = zero, zero
    for m in range(3):
        pltpu.make_async_copy(mast.at[m], mast.at[m], local_sem.at[m]).wait()

        def tile_max(c, carry, m=m):
            near_acc, far_acc = carry
            near = zero
            far = zero
            for i in range(SHARD):
                x = jnp.abs(mast[m, c, i * WIN : (i + 1) * WIN, :])
                inside = jnp.where(i < border, 1.0, 0.0)
                near = jnp.maximum(near, x * inside)
                far = jnp.maximum(far, x * (1.0 - inside))
            here = lane == m * COLS + c
            near_acc = jnp.where(here, jnp.max(near, axis=1, keepdims=True), near_acc)
            far_acc = jnp.where(here, jnp.max(far, axis=1, keepdims=True), far_acc)
            return near_acc, far_acc

        near_max, far_max = lax.fori_loop(0, COLS, tile_max, (near_max, far_max), unroll=4)
    mine[:, :BLOCK] = near_max
    mine[:, BLOCK:] = far_max

    pl.semaphore_wait(barrier, N_TP - 1 + N_FSDP - 1)

    def x1(d):
        return remote(mine, x1r.at[d], x1s.at[d], x1q.at[d], (f, tp_peer(d)))

    each(1, N_TP, lambda d: x1(d).start())

    for load in loads[:3]:
        load.wait()
    row_of = lax.rem(iota((16, HD), 0), 8)
    keep_tile = [jnp.where(row_of == r, 1.0, 0.0).astype(bf16) for r in range(8)]
    keep = [jnp.concatenate([m] * 16, axis=0) for m in keep_tile]
    keep_wide = [jnp.concatenate([m, m], axis=1) for m in keep]
    sub = iota((8, CACHE), 0)
    live = jnp.zeros((8, CACHE), jnp.int32)
    for r in range(8):
        live = jnp.where(sub == r, lengths[r], live)
    alive = (iota((8, CACHE), 1) < live)[None]
    lead = lax.rem(iota((32, 8, 16), 0), 2)
    fresh_col = iota((32, 8, 16), 2)
    fresh_ok = (lax.rem(fresh_col, 8) == iota((32, 8, 16), 1)) & (fresh_col // 8 <= lead)

    def attend(g):
        wide = pl.ds(pl.multiple_of(g * 2048, 2048), 2048)
        cols = pl.ds(pl.multiple_of(g * HD, HD), HD)
        flat = qbuf[:, wide]
        q = jnp.concatenate([flat[:, h * HD : (h + 1) * HD] for h in range(16)], axis=0)
        q_wide = jnp.concatenate([q * keep[r] for r in range(8)], axis=1)
        k_wide = jnp.concatenate([kbuf[r, :, cols] for r in range(8)], axis=1)
        scores = (nt_dot(q_wide, k_wide) * HD**-0.5).reshape(32, 8, CACHE)
        fresh = (nt_dot(q, new_keys[:, cols]) * HD**-0.5).reshape(32, 8, 16)
        peak = jnp.maximum(
            jnp.max(jnp.where(alive, scores, neg_fill), axis=2, keepdims=True),
            jnp.max(jnp.where(fresh_ok, fresh, neg_fill), axis=2, keepdims=True),
        )
        weights = jnp.where(alive, jnp.exp(scores - peak), 0.0)
        fresh_weights = jnp.where(fresh_ok, jnp.exp(jnp.minimum(fresh - peak, 0.0)), 0.0)
        total = jnp.sum(weights, axis=2, keepdims=True) + jnp.sum(
            fresh_weights, axis=2, keepdims=True
        )
        inverse = 1.0 / total
        probs = (weights * inverse).reshape(256, CACHE).astype(bf16)
        fresh_probs = (fresh_weights * inverse).reshape(256, 16).astype(bf16)
        p_wide = jnp.concatenate([probs * keep_wide[r] for r in range(8)], axis=1)
        v_tall = jnp.concatenate([vbuf[r, :, cols] for r in range(8)], axis=0)
        heads = nn_dot(p_wide, v_tall) + nn_dot(fresh_probs, new_values[:, cols])
        heads = heads.astype(bf16)
        for half in range(2):
            parts = [heads[(half * 8 + h) * 16 : (half * 8 + h + 1) * 16] for h in range(8)]
            sendh[2 * g + half] = jnp.concatenate(parts, axis=1)

    each(0, 2, attend)

    each(1, N_TP, lambda d: x1(d).wait_recv())
    group = mine[...]
    for d in range(1, N_TP):
        group = jnp.maximum(group, x1r[d])
    every[f] = group

    def x2(d):
        return remote(
            every.at[f], every.at[f], x2s.at[d], x2q.at[d], (lax.rem(f + d, N_FSDP), t)
        )

    each(1, N_FSDP, lambda d: x2(d).start())

    each(2, KVH, attend)

    def send_heads(d):
        return remote(
            sendh.at[tp_peer(d)], recvh.at[t], hs.at[d], hq.at[d], (f, tp_peer(d))
        )

    each(1, N_TP, lambda d: send_heads(d).start())
    recvh[t] = sendh[t]

    each(1, N_FSDP, lambda d: x2(d).wait_recv())
    for tile in range(TILES):
        parts = []
        for owner in range(N_FSDP):
            first = owner * N_TP * SHARD // BLOCK
            last = (owner * N_TP * SHARD + N_TP * SHARD - 1) // BLOCK
            if first == tile:
                parts.append(every[owner, :, :BLOCK])
            if last == tile and last != first:
                parts.append(every[owner, :, BLOCK:])
        tile_maxima = parts[0]
        for part in parts[1:]:
            tile_maxima = jnp.maximum(tile_maxima, part)
        bm[tile] = tile_maxima
        log = jnp.log2((tile_maxima + epsilon) / fp_limit)
        for m in range(3):
            logs[m, tile] = log[:, m * COLS : (m + 1) * COLS]

    scales = [
        (bm[first_tile] + epsilon) / fp_limit,
        (bm[jnp.minimum(first_tile + 1, TILES - 1)] + epsilon) / fp_limit,
    ]
    inverses = [tie_nudge / scale for scale in scales]

    for m in range(3):

        def restore(c, carry, m=m):
            here = lane == m * COLS + c
            near_scale, far_scale, near_inv, far_inv = (
                jnp.sum(jnp.where(here, table, 0.0), axis=1, keepdims=True)
                for table in scales + inverses
            )
            for i in range(SHARD):
                rows = slice(i * WIN, (i + 1) * WIN)
                value = mast[m, c, rows, :] * jnp.where(i < border, near_inv, far_inv)
                grid = value.astype(jnp.float8_e4m3fn).astype(f32)
                mast[m, c, rows, :] = grid * jnp.where(i < border, near_scale, far_scale)
            return carry

        lax.fori_loop(0, COLS, restore, 0, unroll=2)

    def quantize(e, d):
        for m in range(3):

            def piece(c, carry, m=m):
                parts = [
                    mast[m, quarter * (QUARTER // BLOCK) + c, pl.ds(e, SHARD, stride=WIN), :]
                    for quarter in range(4)
                ]
                cols = pl.ds(pl.multiple_of(c * BLOCK, BLOCK), BLOCK)
                sendw[d, m, :, cols] = jnp.concatenate(parts, axis=0).astype(bf16)
                return carry

            lax.fori_loop(0, QUARTER // BLOCK, piece, 0, unroll=4)

    def send_weights(d):
        return remote(
            sendw.at[d], wbuf.at[0, :, t], ws.at[d], wq.at[d], (f, tp_peer(d))
        )

    def convert(d):
        quantize(tp_peer(d), d)
        send_weights(d).start()

    each(1, N_TP, convert)

    def pass_on(d):
        origin = lax.rem(t + N_TP - d, N_TP)
        return remote(
            wbuf.at[0, :, origin], wbuf.at[1, :, origin], cs.at[d], cq.at[d], (partner, t)
        )

    quantize(t, 0)
    for m in range(3):
        wbuf[0, m, t] = sendw[0, m]
    pass_on(0).start()

    loads[4].wait()
    each(1, N_TP, lambda d: send_heads(d).wait_recv())

    def send_projected(s, d):
        return remote(
            sendp.at[s, d], recvp.at[s, t], ps.at[s, d], pq.at[s, d], (f, tp_peer(d))
        )

    def project(i):
        d = lax.rem(i, N_TP)
        cols = pl.ds(pl.multiple_of(tp_peer(d) * SHARE, SHARE), SHARE)
        rows = recvh[...].reshape(STEPS * ROWS, QH * HD // N_TP)
        result = nn_dot(rows, wproj[:, cols]).reshape(8, STEPS, 8, SHARE)
        for s in range(STEPS):
            sendp[s, d] = result[:, s].reshape(ROWS, SHARE).astype(bf16)

        @pl.when(d != 0)
        def _():
            for s in range(STEPS):
                send_projected(s, d).start()

    each(1, N_TP + 1, project)
    for s in range(STEPS):
        recvp[s, t] = sendp[s, 0]
    loads[3].wait()

    quarter_of = lax.rem(iota((WIN * CAP, 8 * FOLD), 1), FOLD) // SHARD
    own_share = pl.ds(pl.multiple_of(t * CAP, CAP), CAP)

    def send_slots(s, d):
        return remote(
            sendd.at[s, tp_peer(d)], recvd.at[s, t], ds.at[s, d], dq.at[s, d], (f, tp_peer(d))
        )

    def send_normed(s, d):
        to = 2 * chip_peer(d) + core
        return remote(sende.at[s], recve.at[s, k], es.at[s, d], eq.at[s, d], (to, t))

    def send_partial(s, d):
        to = 2 * chip_peer(d) + core
        return remote(
            sendg.at[s, chip_peer(d)], recvg.at[s, k], gs.at[s, d], gq.at[s, d], (to, t)
        )

    def send_back(s, d):
        return remote(
            sendr.at[s, tp_peer(d)], recvr.at[s, t], rs.at[s, d], rq.at[s, d], (f, tp_peer(d))
        )

    def gathered(s, half, m):
        rows = recve[s].reshape(128, 2048)
        rows = jnp.concatenate([rows[:, :QUARTER], rows[:, QUARTER:]], axis=0)
        product = nt_dot(rows, wbuf[half, m].reshape(8 * FOLD, QUARTER))
        product = product.reshape(2, 8, 2, CAP, 8 * FOLD)
        by = [product[q % 2, :, q // 2].reshape(WIN * CAP, 8 * FOLD) for q in range(4)]
        parts = jnp.where(
            quarter_of == 0,
            by[0],
            jnp.where(quarter_of == 1, by[1], jnp.where(quarter_of == 2, by[2], by[3])),
        )
        high = parts.astype(bf16)
        rest = parts - high.astype(f32)
        middle = rest.astype(bf16)
        low = (rest - middle.astype(f32)).astype(bf16)
        split = nn_dot(jnp.concatenate([high, middle, low], axis=0), spread[...])
        split = split.reshape(3, WIN * CAP, 8 * FOLD)
        return split[0] + split[1] + split[2]

    def decode(s):
        each(1, N_TP, lambda d: send_projected(s, d).wait_recv())
        projected = recvp[s, 0].astype(f32)
        for j in range(1, N_TP):
            projected = projected + recvp[s, j].astype(f32)
        mix = (cur[...].astype(f32) + projected).astype(bf16)
        mixed[s] = mix
        sendd[s] = nn_dot(slots[s], mix).reshape(WIN, CAP, SHARE)
        each(1, N_TP, lambda d: send_slots(s, d).start())
        recvd[s, t] = sendd[s, t]
        each(1, N_TP, lambda d: send_slots(s, d).wait_recv())
        blocks = [recvd[s, j] for j in range(N_TP)]
        squares = blocks[0] * blocks[0]
        for block in blocks[1:]:
            squares = squares + block * block
        squares = jnp.sum(squares, axis=1, keepdims=True)
        inverse = lax.rsqrt(squares * (1.0 / D) + epsilon)
        normed = [
            blocks[j] * inverse * gain[:, j * SHARE : (j + 1) * SHARE] for j in range(N_TP)
        ]
        folded = jnp.concatenate(
            [jnp.concatenate(normed[:4], axis=1), jnp.concatenate(normed[4:], axis=1)], axis=0
        ).astype(bf16)
        sende[s] = folded
        each(1, 8, lambda d: send_normed(s, d).start())
        recve[s, k] = folded

        @pl.when(s == 0)
        def _():
            def forward(d):
                send_weights(d).wait_recv()
                pass_on(d).start()

            each(1, N_TP, forward)
            each(0, N_TP, lambda d: pass_on(d).wait_recv())

        each(1, 8, lambda d: send_normed(s, d).wait_recv())
        total = jnp.zeros((4 * WIN * CAP, QUARTER), f32)
        for half in range(2):
            gate = gathered(s, half, 0)
            up = gathered(s, half, 1)
            act = gate / (1.0 + jnp.exp(-gate)) * up
            stacked = jnp.concatenate(
                [jnp.where(quarter_of == q, act, 0.0) for q in range(4)], axis=0
            ).astype(bf16)
            total = total + nn_dot(stacked, wbuf[half, 2].reshape(8 * FOLD, QUARTER))
        total = total.reshape(4, 8, CAP, QUARTER)
        halves = [jnp.concatenate([total[2 * h], total[2 * h + 1]], axis=2) for h in range(2)]
        sendg[s] = jnp.concatenate(halves, axis=1).astype(bf16)
        each(1, 8, lambda d: send_partial(s, d).start())
        recvg[s, k] = sendg[s, k]
        each(1, 8, lambda d: send_partial(s, d).wait_recv())
        summed = recvg[s, 0].astype(f32)
        for j in range(1, 8):
            summed = summed + recvg[s, j].astype(f32)
        summed = summed.reshape(2, CAP, 2048) * share[s, own_share, :1][None]
        for j in range(N_TP):
            sendr[s, j] = summed[j // 4, :, (j % 4) * SHARE : (j % 4 + 1) * SHARE]
        each(1, N_TP, lambda d: send_back(s, d).start())
        recvr[s, t] = sendr[s, t]
        each(1, N_TP, lambda d: send_back(s, d).wait_recv())
        returned = recvr[s].reshape(WIN * CAP, SHARE).astype(bf16)
        moe = nn_dot(slots_t[s], returned)
        cur[...] = (mixed[s].astype(f32) + moe).astype(bf16)

    each(0, STEPS, decode)
    out[...] = cur[...]

    each(1, N_FSDP, lambda d: x2(d).wait_send())
    each(0, N_TP, lambda d: pass_on(d).wait_send())

    def drain(d):
        x1(d).wait_send()
        send_heads(d).wait_send()
        send_weights(d).wait_send()
        for s in range(STEPS):
            send_projected(s, d).wait_send()
            send_slots(s, d).wait_send()
            send_normed(s, d).wait_send()
            send_partial(s, d).wait_send()
            send_back(s, d).wait_send()

    each(1, N_TP, drain)


def local(
    hidden_in,
    queries,
    key_cache,
    value_cache,
    new_keys,
    new_values,
    lengths,
    routes,
    route_weights,
    norm_gain,
    gate_master,
    up_master,
    down_master,
    out_proj,
):
    def flat(master):
        return master.transpose(1, 0, 2).reshape(SHARD * WIN, D)

    vmem = pl.BlockSpec(memory_space=pltpu.VMEM)
    smem = pl.BlockSpec(memory_space=pltpu.SMEM)
    far = pl.BlockSpec(memory_space=pl.ANY)
    dma = pltpu.SemaphoreType.DMA
    v = pltpu.VMEM
    scratch = [
        v((3, COLS, SHARD * WIN, BLOCK), f32),
        v((16, QH * HD), bf16),
        v((8, CACHE, KVH * HD), bf16),
        v((8, CACHE, KVH * HD), bf16),
        v((QH * HD // N_TP, D), bf16),
        v((ROWS, SHARE), bf16),
        v((WIN, 2 * BLOCK), f32),
        v((N_TP, WIN, 2 * BLOCK), f32),
        v((N_FSDP, WIN, 2 * BLOCK), f32),
        v((TILES, WIN, BLOCK), f32),
        v((N_TP, 3, FOLD, QUARTER), bf16),
        v((2, 3, N_TP, FOLD, QUARTER), bf16),
        v((N_TP, 16, 1024), bf16),
        v((N_TP, 16, 1024), bf16),
        v((STEPS, N_TP, ROWS, SHARE), bf16),
        v((STEPS, N_TP, ROWS, SHARE), bf16),
        v((STEPS, WIN * CAP, ROWS), bf16),
        v((STEPS, ROWS, WIN * CAP), bf16),
        v((STEPS, WIN * CAP, BLOCK), f32),
        v((STEPS, ROWS, SHARE), bf16),
        v((STEPS, WIN, CAP, SHARE), f32),
        v((STEPS, N_TP, CAP, SHARE), f32),
        v((STEPS, 16, 2048), bf16),
        v((STEPS, 8, 16, 2048), bf16),
        v((STEPS, 8, 16, 2048), bf16),
        v((STEPS, 8, 16, 2048), bf16),
        v((STEPS, N_TP, CAP, SHARE), f32),
        v((STEPS, N_TP, CAP, SHARE), f32),
        v((8 * FOLD, 8 * FOLD), bf16),
        dma((8,)),
        dma((N_TP,)),
        dma((N_TP,)),
        dma((N_FSDP,)),
        dma((N_FSDP,)),
    ]
    scratch += [dma((N_TP,)) for _ in range(6)]
    scratch += [dma((STEPS, N_TP)) for _ in range(10)]
    out, logs = pl.pallas_call(
        kernel,
        out_shape=(
            jax.ShapeDtypeStruct((ROWS, SHARE), bf16),
            jax.ShapeDtypeStruct((3, TILES, WIN, COLS), f32),
        ),
        in_specs=[far, far, far, far, vmem, vmem, smem, vmem, vmem, vmem, far, far, far, far],
        out_specs=(vmem, vmem),
        scratch_shapes=scratch,
        compiler_params=pltpu.CompilerParams(
            collective_id=0, has_side_effects=True, vmem_limit_bytes=58 << 20
        ),
    )(
        hidden_in,
        queries.reshape(16, QH * HD),
        key_cache,
        value_cache,
        new_keys.reshape(16, KVH * HD),
        new_values.reshape(16, KVH * HD),
        lengths,
        routes.transpose(0, 2, 1),
        route_weights.transpose(0, 2, 1),
        norm_gain.reshape(1, D),
        flat(gate_master),
        flat(up_master),
        flat(down_master),
        out_proj,
    )
    return (out, logs.transpose(0, 2, 1, 3))


def solution(mesh):
    in_specs = (
        P("fsdp", None),
        P(None, ("fsdp", "tp"), None),
        P(("fsdp", "tp"), None, None),
        P(("fsdp", "tp"), None, None),
        P(None, ("fsdp", "tp"), None),
        P(None, ("fsdp", "tp"), None),
        P(("fsdp", "tp")),
        P(None, "fsdp", None),
        P(None, "fsdp", None),
        P(),
        P(None, ("fsdp", "tp"), None),
        P(None, ("fsdp", "tp"), None),
        P(None, ("fsdp", "tp"), None),
        P("tp", None),
    )
    out_specs = (P("fsdp", "tp"), P())
    return jax.shard_map(local, mesh=mesh, in_specs=in_specs, out_specs=out_specs, check_vma=False)
```

```python
import jax
import jax.numpy as jnp
from jax import lax
from jax.experimental import pallas as pl
from jax.experimental.pallas import tpu as pltpu
from jax.sharding import PartitionSpec as P

D = 4096
FF = 1536
QH = 64
KVH = 4
HD = 128
BLOCK = 128
WIN = 8
CAP = 8
STEPS = 2
ROWS = 64
CACHE = 256
N_FSDP = 16
N_TP = 8
SHARD = FF // (N_FSDP * N_TP)
TILES = FF // BLOCK
COLS = D // BLOCK
SHARE = D // N_TP
NEAR = 4 * N_TP
QUARTER = D // 4
FOLD = 4 * SHARD

neg_fill = -1e30
epsilon = 1e-06
fp_limit = 448.0
tie_nudge = 1.0 + 2.0**-22

f32 = jnp.float32
bf16 = jnp.bfloat16


def nt_dot(a, b):
    return lax.dot_general(a, b, (((1,), (1,)), ((), ())), preferred_element_type=f32)


def nn_dot(a, b):
    return lax.dot_general(a, b, (((1,), (0,)), ((), ())), preferred_element_type=f32)


def iota(shape, dim):
    return lax.broadcasted_iota(jnp.int32, shape, dim)


def kernel(
    hidden,
    queries,
    key_cache,
    value_cache,
    new_keys,
    new_values,
    lengths,
    routes,
    route_weights,
    gain,
    gate_master,
    up_master,
    down_master,
    out_proj,
    out,
    logs,
    mast,
    qbuf,
    kbuf,
    vbuf,
    wproj,
    cur,
    mine,
    x1r,
    every,
    sendw,
    wbuf,
    sendh,
    recvh,
    sendp,
    recvp,
    slots,
    slots_t,
    share,
    mixed,
    sendd,
    recvd,
    sende,
    recve,
    sendg,
    recvg,
    sendr,
    recvr,
    spread,
    local_sem,
    x1s,
    x1q,
    x2s,
    x2q,
    hs,
    hq,
    ws,
    wq,
    cs,
    cq,
    ps,
    pq,
    ds,
    dq,
    es,
    eq,
    gs,
    gq,
    rs,
    rq,
):
    f = lax.axis_index("fsdp")
    t = lax.axis_index("tp")
    k = f // 2
    core = lax.rem(f, 2)
    partner = f + 1 - 2 * core

    def tp_peer(d):
        return lax.rem(t + d, N_TP)

    def chip_peer(d):
        return lax.rem(k + d, 8)

    def remote(src, dst, send, recv, to):
        return pltpu.make_async_remote_copy(
            src_ref=src,
            dst_ref=dst,
            send_sem=send,
            recv_sem=recv,
            device_id=to,
            device_id_type=pl.DeviceIdType.MESH,
        )

    def each(low, high, body):
        def step(d, carry):
            body(d)
            return carry

        lax.fori_loop(low, high, step, 0)

    barrier = pltpu.get_barrier_semaphore()

    def greet(to):
        pl.semaphore_signal(barrier, inc=1, device_id=to, device_id_type=pl.DeviceIdType.MESH)

    def near_peer(d):
        return (f // 4) * 4 + lax.rem(lax.rem(f, 4) + d // N_TP, 4), lax.rem(t + d, N_TP)

    def far_peer(d):
        return 4 * lax.rem(f // 4 + 1 + d // 2, 4) + 2 * lax.rem(d, 2) + core, t

    each(1, NEAR, lambda d: greet(near_peer(d)))
    each(0, 6, lambda d: greet(far_peer(d)))

    own_cols = pl.ds(pl.multiple_of(t * SHARE, SHARE), SHARE)
    loads = [
        pltpu.make_async_copy(queries, qbuf, local_sem.at[3]),
        pltpu.make_async_copy(key_cache, kbuf, local_sem.at[4]),
        pltpu.make_async_copy(value_cache, vbuf, local_sem.at[5]),
        pltpu.make_async_copy(hidden.at[:, own_cols], cur, local_sem.at[6]),
        pltpu.make_async_copy(out_proj, wproj, local_sem.at[7]),
    ]
    for m, master in enumerate((gate_master, up_master, down_master)):

        def load_rows(i, m=m, master=master):
            rows = pl.ds(pl.multiple_of(i * WIN, WIN), WIN)
            pltpu.make_async_copy(master.at[i], mast.at[m, :, rows], local_sem.at[m]).start()

        each(0, SHARD, load_rows)
    for load in loads:
        load.start()

    lane64 = iota((ROWS, ROWS), 1)
    row64 = iota((ROWS, ROWS), 0)
    earlier = (row64 < lane64).astype(f32).astype(bf16)
    expert_rows = iota((WIN, ROWS), 0)
    for s in range(STEPS):
        names = routes[s]
        weights = route_weights[s]
        total = jnp.sum(weights, axis=0, keepdims=True)
        chosen = jnp.zeros((WIN, ROWS), f32)
        shares = jnp.zeros((WIN, ROWS), f32)
        for e in range(WIN):
            match = names == e
            has = jnp.max(jnp.where(match, 1.0, 0.0), axis=0, keepdims=True)
            sums = jnp.sum(jnp.where(match, weights, 0.0), axis=0, keepdims=True)
            chosen = jnp.where(expert_rows == e, has, chosen)
            shares = jnp.where(expert_rows == e, sums, shares)
        shares = shares / total
        place = nn_dot(chosen.astype(bf16), earlier)
        place = jnp.where(chosen > 0.5, place, 1000.0)
        place_index = iota((WIN, CAP, ROWS), 1).astype(f32)
        picked = jnp.where(place[:, None, :] == place_index, 1.0, 0.0)
        picked2 = picked.reshape(WIN * CAP, ROWS)
        slots[s] = picked2.astype(bf16)
        slots_t[s] = picked2.T.astype(bf16)
        slot_share = jnp.sum(picked * shares[:, None, :], axis=2, keepdims=True)
        share[s] = jnp.broadcast_to(slot_share.reshape(WIN * CAP, 1), (WIN * CAP, BLOCK))
    column = iota((8 * FOLD, 8 * FOLD), 1)
    line = iota((8 * FOLD, 8 * FOLD), 0)
    same = ((column // FOLD) == (line // FOLD)) & (lax.rem(column, SHARD) == lax.rem(line, SHARD))
    spread[...] = jnp.where(same, 1.0, 0.0).astype(bf16)

    first_tile = (f * (N_TP * SHARD)) // BLOCK
    first_row = (f * N_TP + t) * SHARD
    border = (first_tile + 1) * BLOCK - first_row
    lane = iota((WIN, BLOCK), 1)
    zero = jnp.zeros((WIN, BLOCK), f32)
    near_max, far_max = zero, zero
    for m in range(3):
        pltpu.make_async_copy(mast.at[m], mast.at[m], local_sem.at[m]).wait()

        def tile_max(c, carry, m=m):
            near_acc, far_acc = carry
            near = zero
            far = zero
            for i in range(SHARD):
                x = jnp.abs(mast[m, c, i * WIN : (i + 1) * WIN, :])
                inside = jnp.where(i < border, 1.0, 0.0)
                near = jnp.maximum(near, x * inside)
                far = jnp.maximum(far, x * (1.0 - inside))
            here = lane == m * COLS + c
            near_acc = jnp.where(here, jnp.max(near, axis=1, keepdims=True), near_acc)
            far_acc = jnp.where(here, jnp.max(far, axis=1, keepdims=True), far_acc)
            return near_acc, far_acc

        near_max, far_max = lax.fori_loop(0, COLS, tile_max, (near_max, far_max), unroll=4)
    mine[:, :BLOCK] = near_max
    mine[:, BLOCK:] = far_max

    pl.semaphore_wait(barrier, NEAR - 1 + 6)

    place_here = lax.rem(f, 4) * N_TP + t

    def x1(d):
        return remote(mine, x1r.at[place_here], x1s.at[d], x1q.at[d], near_peer(d))

    each(1, NEAR, lambda d: x1(d).start())
    x1r[place_here] = mine[...]

    for load in loads[:3]:
        load.wait()
    row_of = lax.rem(iota((16, HD), 0), 8)
    keep_tile = [jnp.where(row_of == r, 1.0, 0.0).astype(bf16) for r in range(8)]
    keep = [jnp.concatenate([m] * 16, axis=0) for m in keep_tile]
    keep_wide = [jnp.concatenate([m, m], axis=1) for m in keep]
    sub = iota((8, CACHE), 0)
    live = jnp.zeros((8, CACHE), jnp.int32)
    for r in range(8):
        live = jnp.where(sub == r, lengths[r], live)
    alive = (iota((8, CACHE), 1) < live)[None]
    lead = lax.rem(iota((32, 8, 16), 0), 2)
    fresh_col = iota((32, 8, 16), 2)
    fresh_ok = (lax.rem(fresh_col, 8) == iota((32, 8, 16), 1)) & (fresh_col // 8 <= lead)

    def attend(g):
        wide = pl.ds(pl.multiple_of(g * 2048, 2048), 2048)
        cols = pl.ds(pl.multiple_of(g * HD, HD), HD)
        flat = qbuf[:, wide]
        q = jnp.concatenate([flat[:, h * HD : (h + 1) * HD] for h in range(16)], axis=0)
        q_wide = jnp.concatenate([q * keep[r] for r in range(8)], axis=1)
        k_wide = jnp.concatenate([kbuf[r, :, cols] for r in range(8)], axis=1)
        scores = (nt_dot(q_wide, k_wide) * HD**-0.5).reshape(32, 8, CACHE)
        fresh = (nt_dot(q, new_keys[:, cols]) * HD**-0.5).reshape(32, 8, 16)
        peak = jnp.maximum(
            jnp.max(jnp.where(alive, scores, neg_fill), axis=2, keepdims=True),
            jnp.max(jnp.where(fresh_ok, fresh, neg_fill), axis=2, keepdims=True),
        )
        weights = jnp.where(alive, jnp.exp(scores - peak), 0.0)
        fresh_weights = jnp.where(fresh_ok, jnp.exp(jnp.minimum(fresh - peak, 0.0)), 0.0)
        total = jnp.sum(weights, axis=2, keepdims=True) + jnp.sum(
            fresh_weights, axis=2, keepdims=True
        )
        inverse = 1.0 / total
        probs = (weights * inverse).reshape(256, CACHE).astype(bf16)
        fresh_probs = (fresh_weights * inverse).reshape(256, 16).astype(bf16)
        p_wide = jnp.concatenate([probs * keep_wide[r] for r in range(8)], axis=1)
        v_tall = jnp.concatenate([vbuf[r, :, cols] for r in range(8)], axis=0)
        heads = nn_dot(p_wide, v_tall) + nn_dot(fresh_probs, new_values[:, cols])
        heads = heads.astype(bf16)
        for half in range(2):
            parts = [heads[(half * 8 + h) * 16 : (half * 8 + h + 1) * 16] for h in range(8)]
            sendh[2 * g + half] = jnp.concatenate(parts, axis=1)

    each(0, KVH, attend)

    def send_heads(d):
        return remote(
            sendh.at[tp_peer(d)], recvh.at[t], hs.at[d], hq.at[d], (f, tp_peer(d))
        )

    each(1, N_TP, lambda d: send_heads(d).start())
    recvh[t] = sendh[t]

    each(1, NEAR, lambda d: x1(d).wait_recv())
    quad = f // 4
    for tile in range(3):
        first = x1r[tile * N_TP, :, BLOCK if tile else 0 : 2 * BLOCK if tile else BLOCK]
        for j in range(N_TP):
            if tile:
                first = jnp.maximum(first, x1r[tile * N_TP + j, :, BLOCK:])
            else:
                first = jnp.maximum(first, x1r[j, :, :BLOCK])
            first = jnp.maximum(first, x1r[(tile + 1) * N_TP + j, :, :BLOCK])
        every[quad, tile] = first

    def x2(d):
        to = 4 * lax.rem(quad + d, 4) + lax.rem(f, 4)
        return remote(every.at[quad], every.at[quad], x2s.at[d], x2q.at[d], (to, t))

    each(1, 4, lambda d: x2(d).start())

    near_tile = first_tile - 3 * quad
    scales = [
        (every[quad, near_tile] + epsilon) / fp_limit,
        (every[quad, jnp.minimum(near_tile + 1, 2)] + epsilon) / fp_limit,
    ]
    inverses = [tie_nudge / scale for scale in scales]

    def send_weights(m, d):
        return remote(
            sendw.at[m, d], wbuf.at[0, m, t], ws.at[m, d], wq.at[m, d], (f, tp_peer(d))
        )

    def convert_matrix(m):
        def restore(c, carry):
            here = lane == m * COLS + c
            near_scale, far_scale, near_inv, far_inv = (
                jnp.sum(jnp.where(here, table, 0.0), axis=1, keepdims=True)
                for table in scales + inverses
            )
            for i in range(SHARD):
                rows = slice(i * WIN, (i + 1) * WIN)
                value = mast[m, c, rows, :] * jnp.where(i < border, near_inv, far_inv)
                grid = value.astype(jnp.float8_e4m3fn).astype(f32)
                mast[m, c, rows, :] = grid * jnp.where(i < border, near_scale, far_scale)
            return carry

        lax.fori_loop(0, COLS, restore, 0, unroll=2)

        def convert(i):
            d = lax.rem(i, N_TP)
            e = tp_peer(d)

            def piece(c, carry):
                parts = [
                    mast[m, quarter * (QUARTER // BLOCK) + c, pl.ds(e, SHARD, stride=WIN), :]
                    for quarter in range(4)
                ]
                cols = pl.ds(pl.multiple_of(c * BLOCK, BLOCK), BLOCK)
                sendw[m, d, :, cols] = jnp.concatenate(parts, axis=0).astype(bf16)
                return carry

            lax.fori_loop(0, QUARTER // BLOCK, piece, 0, unroll=4)

            @pl.when(d != 0)
            def _():
                send_weights(m, d).start()

        each(1, N_TP + 1, convert)
        wbuf[0, m, t] = sendw[m, 0]

    convert_matrix(0)

    loads[4].wait()
    each(1, N_TP, lambda d: send_heads(d).wait_recv())

    def send_projected(s, d):
        return remote(
            sendp.at[s, d], recvp.at[s, t], ps.at[s, d], pq.at[s, d], (f, tp_peer(d))
        )

    def project(i):
        d = lax.rem(i, N_TP)
        cols = pl.ds(pl.multiple_of(tp_peer(d) * SHARE, SHARE), SHARE)
        rows = recvh[...].reshape(STEPS * ROWS, QH * HD // N_TP)
        result = nn_dot(rows, wproj[:, cols]).reshape(8, STEPS, 8, SHARE)
        for s in range(STEPS):
            sendp[s, d] = result[:, s].reshape(ROWS, SHARE).astype(bf16)

        @pl.when(d != 0)
        def _():
            send_projected(0, d).start()

    each(1, N_TP + 1, project)
    for s in range(STEPS):
        recvp[s, t] = sendp[s, 0]
    loads[3].wait()

    convert_matrix(1)
    convert_matrix(2)

    def pass_on(d):
        origin = lax.rem(t + N_TP - d, N_TP)
        return remote(
            wbuf.at[0, :, origin], wbuf.at[1, :, origin], cs.at[d], cq.at[d], (partner, t)
        )

    pass_on(0).start()

    quarter_of = lax.rem(iota((WIN * CAP, 8 * FOLD), 1), FOLD) // SHARD
    own_share = pl.ds(pl.multiple_of(t * CAP, CAP), CAP)

    def send_slots(s, d):
        return remote(
            sendd.at[s, tp_peer(d)], recvd.at[s, t], ds.at[s, d], dq.at[s, d], (f, tp_peer(d))
        )

    def send_normed(s, d):
        to = 2 * chip_peer(d) + core
        return remote(sende.at[s], recve.at[s, k], es.at[s, d], eq.at[s, d], (to, t))

    def send_partial(s, d):
        to = 2 * chip_peer(d) + core
        return remote(
            sendg.at[s, chip_peer(d)], recvg.at[s, k], gs.at[s, d], gq.at[s, d], (to, t)
        )

    def send_back(s, d):
        return remote(
            sendr.at[s, tp_peer(d)], recvr.at[s, t], rs.at[s, d], rq.at[s, d], (f, tp_peer(d))
        )

    def gathered(s, half, m):
        rows = recve[s].reshape(128, 2048)
        rows = jnp.concatenate([rows[:, :QUARTER], rows[:, QUARTER:]], axis=0)
        product = nt_dot(rows, wbuf[half, m].reshape(8 * FOLD, QUARTER))
        product = product.reshape(2, 8, 2, CAP, 8 * FOLD)
        by = [product[q % 2, :, q // 2].reshape(WIN * CAP, 8 * FOLD) for q in range(4)]
        parts = jnp.where(
            quarter_of == 0,
            by[0],
            jnp.where(quarter_of == 1, by[1], jnp.where(quarter_of == 2, by[2], by[3])),
        )
        high = parts.astype(bf16)
        rest = parts - high.astype(f32)
        middle = rest.astype(bf16)
        low = (rest - middle.astype(f32)).astype(bf16)
        split = nn_dot(jnp.concatenate([high, middle, low], axis=0), spread[...])
        split = split.reshape(3, WIN * CAP, 8 * FOLD)
        return split[0] + split[1] + split[2]

    def decode(s):
        each(1, N_TP, lambda d: send_projected(s, d).wait_recv())
        projected = recvp[s, 0].astype(f32)
        for j in range(1, N_TP):
            projected = projected + recvp[s, j].astype(f32)
        mix = (cur[...].astype(f32) + projected).astype(bf16)
        mixed[s] = mix
        sendd[s] = nn_dot(slots[s], mix).reshape(WIN, CAP, SHARE)
        each(1, N_TP, lambda d: send_slots(s, d).start())
        recvd[s, t] = sendd[s, t]
        each(1, N_TP, lambda d: send_slots(s, d).wait_recv())
        blocks = [recvd[s, j] for j in range(N_TP)]
        squares = blocks[0] * blocks[0]
        for block in blocks[1:]:
            squares = squares + block * block
        squares = jnp.sum(squares, axis=1, keepdims=True)
        inverse = lax.rsqrt(squares * (1.0 / D) + epsilon)
        normed = [
            blocks[j] * inverse * gain[:, j * SHARE : (j + 1) * SHARE] for j in range(N_TP)
        ]
        folded = jnp.concatenate(
            [jnp.concatenate(normed[:4], axis=1), jnp.concatenate(normed[4:], axis=1)], axis=0
        ).astype(bf16)
        sende[s] = folded
        each(1, 8, lambda d: send_normed(s, d).start())
        recve[s, k] = folded

        @pl.when(s == 0)
        def _():
            def forward(d):
                for m in range(3):
                    send_weights(m, d).wait_recv()
                pass_on(d).start()

            each(1, N_TP, forward)
            each(1, N_TP, lambda d: send_projected(1, d).start())
            each(0, N_TP, lambda d: pass_on(d).wait_recv())

        each(1, 8, lambda d: send_normed(s, d).wait_recv())
        total = jnp.zeros((4 * WIN * CAP, QUARTER), f32)
        for half in range(2):
            gate = gathered(s, half, 0)
            up = gathered(s, half, 1)
            act = gate / (1.0 + jnp.exp(-gate)) * up
            stacked = jnp.concatenate(
                [jnp.where(quarter_of == q, act, 0.0) for q in range(4)], axis=0
            ).astype(bf16)
            total = total + nn_dot(stacked, wbuf[half, 2].reshape(8 * FOLD, QUARTER))
        total = total.reshape(4, 8, CAP, QUARTER)
        halves = [jnp.concatenate([total[2 * h], total[2 * h + 1]], axis=2) for h in range(2)]
        sendg[s] = jnp.concatenate(halves, axis=1).astype(bf16)
        each(1, 8, lambda d: send_partial(s, d).start())
        recvg[s, k] = sendg[s, k]
        each(1, 8, lambda d: send_partial(s, d).wait_recv())
        summed = recvg[s, 0].astype(f32)
        for j in range(1, 8):
            summed = summed + recvg[s, j].astype(f32)
        summed = summed.reshape(2, CAP, 2048) * share[s, own_share, :1][None]
        for j in range(N_TP):
            sendr[s, j] = summed[j // 4, :, (j % 4) * SHARE : (j % 4 + 1) * SHARE]
        each(1, N_TP, lambda d: send_back(s, d).start())
        recvr[s, t] = sendr[s, t]
        each(1, N_TP, lambda d: send_back(s, d).wait_recv())
        returned = recvr[s].reshape(WIN * CAP, SHARE).astype(bf16)
        moe = nn_dot(slots_t[s], returned)
        cur[...] = (mixed[s].astype(f32) + moe).astype(bf16)

    each(0, STEPS, decode)
    out[...] = cur[...]

    each(1, 4, lambda d: x2(d).wait_recv())
    for tile in range(TILES):
        log = jnp.log2((every[tile // 3, tile % 3] + epsilon) / fp_limit)
        for m in range(3):
            logs[m, tile] = log[:, m * COLS : (m + 1) * COLS]
    each(1, 4, lambda d: x2(d).wait_send())
    each(1, NEAR, lambda d: x1(d).wait_send())
    each(0, N_TP, lambda d: pass_on(d).wait_send())

    def drain(d):
        send_heads(d).wait_send()
        for m in range(3):
            send_weights(m, d).wait_send()
        for s in range(STEPS):
            send_projected(s, d).wait_send()
            send_slots(s, d).wait_send()
            send_normed(s, d).wait_send()
            send_partial(s, d).wait_send()
            send_back(s, d).wait_send()

    each(1, N_TP, drain)


def local(
    hidden_in,
    queries,
    key_cache,
    value_cache,
    new_keys,
    new_values,
    lengths,
    routes,
    route_weights,
    norm_gain,
    gate_master,
    up_master,
    down_master,
    out_proj,
):
    def flat(master):
        blocks = master.transpose(1, 0, 2).reshape(SHARD, WIN, COLS, BLOCK)
        return blocks.transpose(0, 2, 1, 3)

    vmem = pl.BlockSpec(memory_space=pltpu.VMEM)
    smem = pl.BlockSpec(memory_space=pltpu.SMEM)
    far = pl.BlockSpec(memory_space=pl.ANY)
    dma = pltpu.SemaphoreType.DMA
    v = pltpu.VMEM
    scratch = [
        v((3, COLS, SHARD * WIN, BLOCK), f32),
        v((16, QH * HD), bf16),
        v((8, CACHE, KVH * HD), bf16),
        v((8, CACHE, KVH * HD), bf16),
        v((QH * HD // N_TP, D), bf16),
        v((ROWS, SHARE), bf16),
        v((WIN, 2 * BLOCK), f32),
        v((NEAR, WIN, 2 * BLOCK), f32),
        v((4, 3, WIN, BLOCK), f32),
        v((3, N_TP, FOLD, QUARTER), bf16),
        v((2, 3, N_TP, FOLD, QUARTER), bf16),
        v((N_TP, 16, 1024), bf16),
        v((N_TP, 16, 1024), bf16),
        v((STEPS, N_TP, ROWS, SHARE), bf16),
        v((STEPS, N_TP, ROWS, SHARE), bf16),
        v((STEPS, WIN * CAP, ROWS), bf16),
        v((STEPS, ROWS, WIN * CAP), bf16),
        v((STEPS, WIN * CAP, BLOCK), f32),
        v((STEPS, ROWS, SHARE), bf16),
        v((STEPS, WIN, CAP, SHARE), f32),
        v((STEPS, N_TP, CAP, SHARE), f32),
        v((STEPS, 16, 2048), bf16),
        v((STEPS, 8, 16, 2048), bf16),
        v((STEPS, 8, 16, 2048), bf16),
        v((STEPS, 8, 16, 2048), bf16),
        v((STEPS, N_TP, CAP, SHARE), f32),
        v((STEPS, N_TP, CAP, SHARE), f32),
        v((8 * FOLD, 8 * FOLD), bf16),
        dma((8,)),
        dma((NEAR,)),
        dma((NEAR,)),
        dma((4,)),
        dma((4,)),
        dma((N_TP,)),
        dma((N_TP,)),
        dma((3, N_TP)),
        dma((3, N_TP)),
        dma((N_TP,)),
        dma((N_TP,)),
    ]
    scratch += [dma((STEPS, N_TP)) for _ in range(10)]
    out, logs = pl.pallas_call(
        kernel,
        out_shape=(
            jax.ShapeDtypeStruct((ROWS, SHARE), bf16),
            jax.ShapeDtypeStruct((3, TILES, WIN, COLS), f32),
        ),
        in_specs=[far, far, far, far, vmem, vmem, smem, vmem, vmem, vmem, far, far, far, far],
        out_specs=(vmem, vmem),
        scratch_shapes=scratch,
        compiler_params=pltpu.CompilerParams(
            collective_id=0, has_side_effects=True, vmem_limit_bytes=58 << 20
        ),
    )(
        hidden_in,
        queries.reshape(16, QH * HD),
        key_cache,
        value_cache,
        new_keys.reshape(16, KVH * HD),
        new_values.reshape(16, KVH * HD),
        lengths,
        routes.transpose(0, 2, 1),
        route_weights.transpose(0, 2, 1),
        norm_gain.reshape(1, D),
        flat(gate_master),
        flat(up_master),
        flat(down_master),
        out_proj,
    )
    return (out, logs.transpose(0, 2, 1, 3))


def solution(mesh):
    in_specs = (
        P("fsdp", None),
        P(None, ("fsdp", "tp"), None),
        P(("fsdp", "tp"), None, None),
        P(("fsdp", "tp"), None, None),
        P(None, ("fsdp", "tp"), None),
        P(None, ("fsdp", "tp"), None),
        P(("fsdp", "tp")),
        P(None, "fsdp", None),
        P(None, "fsdp", None),
        P(),
        P(None, ("fsdp", "tp"), None),
        P(None, ("fsdp", "tp"), None),
        P(None, ("fsdp", "tp"), None),
        P("tp", None),
    )
    out_specs = (P("fsdp", "tp"), P())
    return jax.shard_map(local, mesh=mesh, in_specs=in_specs, out_specs=out_specs, check_vma=False)
```

```python
import jax
import jax.numpy as jnp
from jax import lax
from jax.experimental import pallas as pl
from jax.experimental.pallas import tpu as pltpu
from jax.sharding import PartitionSpec as P

D = 4096
FF = 1536
QH = 64
KVH = 4
HD = 128
BLOCK = 128
WIN = 8
CAP = 8
STEPS = 2
ROWS = 64
CACHE = 256
N_FSDP = 16
N_TP = 8
SHARD = FF // (N_FSDP * N_TP)
TILES = FF // BLOCK
COLS = D // BLOCK
SHARE = D // N_TP
NEAR = 2 * N_TP
MATES = 8 * N_TP
QUARTER = D // 4
FOLD = 4 * SHARD

neg_fill = -1e30
epsilon = 1e-06
fp_limit = 448.0
EARLY = 1
tie_nudge = 1.0 + 2.0**-22

f32 = jnp.float32
bf16 = jnp.bfloat16


def nt_dot(a, b):
    return lax.dot_general(a, b, (((1,), (1,)), ((), ())), preferred_element_type=f32)


def nn_dot(a, b):
    return lax.dot_general(a, b, (((1,), (0,)), ((), ())), preferred_element_type=f32)


def iota(shape, dim):
    return lax.broadcasted_iota(jnp.int32, shape, dim)


def kernel(
    hidden,
    queries,
    key_cache,
    value_cache,
    new_keys,
    new_values,
    lengths,
    routes,
    route_weights,
    gain,
    gate_master,
    up_master,
    down_master,
    out_proj,
    out,
    logs,
    mast,
    qbuf,
    kbuf,
    vbuf,
    wproj,
    cur,
    mine,
    other,
    both,
    x1r,
    every,
    sendw,
    wbuf,
    sendh,
    recvh,
    sendp,
    recvp,
    slots,
    slots_t,
    share,
    mixed,
    sendd,
    recvd,
    sende,
    recve,
    sendg,
    recvg,
    spread,
    local_sem,
    x0s,
    x0q,
    x1s,
    x1q,
    x2s,
    x2q,
    hs,
    hq,
    ws,
    wq,
    cs,
    cq,
    ps,
    pq,
    ds,
    dq,
    es,
    eq,
    gs,
    gq,
):
    f = lax.axis_index("fsdp")
    t = lax.axis_index("tp")
    k = f // 2
    core = lax.rem(f, 2)
    partner = f + 1 - 2 * core

    tp_peers = [lax.rem(t + d, N_TP) for d in range(N_TP)]
    chip_peers = [lax.rem(k + d, 8) for d in range(8)]

    def tp_peer(d):
        return tp_peers[d] if isinstance(d, int) else lax.rem(t + d, N_TP)

    def chip_peer(d):
        return chip_peers[d] if isinstance(d, int) else lax.rem(k + d, 8)

    def remote(src, dst, send, recv, to):
        return pltpu.make_async_remote_copy(
            src_ref=src,
            dst_ref=dst,
            send_sem=send,
            recv_sem=recv,
            device_id=to,
            device_id_type=pl.DeviceIdType.MESH,
        )

    def each(low, high, body):
        def step(d, carry):
            body(d)
            return carry

        lax.fori_loop(low, high, step, 0)

    def unrolled(low, high, body):
        for d in range(low, high):
            body(d)

    barrier = pltpu.get_barrier_semaphore()

    def greet(to):
        pl.semaphore_signal(barrier, inc=1, device_id=to, device_id_type=pl.DeviceIdType.MESH)

    def mate(d):
        return 2 * chip_peer(d // N_TP) + core, tp_peer(d % N_TP)

    def near_peer(d):
        side = lax.rem(k, 2)
        chip = k + (d // N_TP) * (1 - 2 * side)
        return 2 * chip + core, tp_peer(d % N_TP)

    unrolled(1, MATES, lambda d: greet(mate(d)))
    greet((partner, t))

    own_cols = pl.ds(pl.multiple_of(t * SHARE, SHARE), SHARE)
    loads = [
        pltpu.make_async_copy(queries, qbuf, local_sem.at[3]),
        pltpu.make_async_copy(key_cache, kbuf, local_sem.at[4]),
        pltpu.make_async_copy(value_cache, vbuf, local_sem.at[5]),
        pltpu.make_async_copy(hidden.at[:, own_cols], cur, local_sem.at[6]),
        pltpu.make_async_copy(out_proj, wproj, local_sem.at[7]),
    ]
    for m, master in enumerate((gate_master, up_master, down_master)):

        def load_rows(i, m=m, master=master):
            rows = pl.ds(pl.multiple_of(i * WIN, WIN), WIN)
            pltpu.make_async_copy(master.at[i], mast.at[m, :, rows], local_sem.at[m]).start()

        each(0, SHARD, load_rows)
    for load in loads:
        load.start()

    lane64 = iota((ROWS, ROWS), 1)
    row64 = iota((ROWS, ROWS), 0)
    earlier = (row64 < lane64).astype(f32).astype(bf16)
    expert_rows = iota((WIN, ROWS), 0)
    for s in range(STEPS):
        names = routes[s]
        weights = route_weights[s]
        total = jnp.sum(weights, axis=0, keepdims=True)
        chosen = jnp.zeros((WIN, ROWS), f32)
        shares = jnp.zeros((WIN, ROWS), f32)
        for e in range(WIN):
            match = names == e
            has = jnp.max(jnp.where(match, 1.0, 0.0), axis=0, keepdims=True)
            sums = jnp.sum(jnp.where(match, weights, 0.0), axis=0, keepdims=True)
            chosen = jnp.where(expert_rows == e, has, chosen)
            shares = jnp.where(expert_rows == e, sums, shares)
        shares = shares / total
        place = nn_dot(chosen.astype(bf16), earlier)
        place = jnp.where(chosen > 0.5, place, 1000.0)
        place_index = iota((WIN, CAP, ROWS), 1).astype(f32)
        picked = jnp.where(place[:, None, :] == place_index, 1.0, 0.0)
        picked2 = picked.reshape(WIN * CAP, ROWS)
        slots[s] = picked2.astype(bf16)
        slots_t[s] = picked2.T.astype(bf16)
        slot_share = jnp.sum(picked * shares[:, None, :], axis=2, keepdims=True)
        share[s] = jnp.broadcast_to(slot_share.reshape(WIN * CAP, 1), (WIN * CAP, BLOCK))
    column = iota((8 * FOLD, 8 * FOLD), 1)
    line = iota((8 * FOLD, 8 * FOLD), 0)
    same = ((column // FOLD) == (line // FOLD)) & (lax.rem(column, SHARD) == lax.rem(line, SHARD))
    spread[...] = jnp.where(same, 1.0, 0.0).astype(bf16)

    first_tile = (f * (N_TP * SHARD)) // BLOCK
    first_row = (f * N_TP + t) * SHARD
    border = (first_tile + 1) * BLOCK - first_row
    lane = iota((WIN, BLOCK), 1)
    zero = jnp.zeros((WIN, BLOCK), f32)
    near_max, far_max = zero, zero
    for m in range(3):
        pltpu.make_async_copy(mast.at[m], mast.at[m], local_sem.at[m]).wait()

        def tile_max(c, carry, m=m):
            near_acc, far_acc = carry
            near = zero
            far = zero
            for i in range(SHARD):
                x = jnp.abs(mast[m, c, i * WIN : (i + 1) * WIN, :])
                inside = jnp.where(i < border, 1.0, 0.0)
                near = jnp.maximum(near, x * inside)
                far = jnp.maximum(far, x * (1.0 - inside))
            here = lane == m * COLS + c
            near_acc = jnp.where(here, jnp.max(near, axis=1, keepdims=True), near_acc)
            far_acc = jnp.where(here, jnp.max(far, axis=1, keepdims=True), far_acc)
            return near_acc, far_acc

        near_max, far_max = lax.fori_loop(0, COLS, tile_max, (near_max, far_max), unroll=4)
    mine[:, :BLOCK] = near_max
    mine[:, BLOCK:] = far_max

    for load in loads[:3]:
        load.wait()
    row_of = lax.rem(iota((16, HD), 0), 8)
    keep_tile = [jnp.where(row_of == r, 1.0, 0.0).astype(bf16) for r in range(8)]
    keep = [jnp.concatenate([m] * 16, axis=0) for m in keep_tile]
    keep_wide = [jnp.concatenate([m, m], axis=1) for m in keep]
    sub = iota((8, CACHE), 0)
    live = jnp.zeros((8, CACHE), jnp.int32)
    for r in range(8):
        live = jnp.where(sub == r, lengths[r], live)
    alive = (iota((8, CACHE), 1) < live)[None]
    lead = lax.rem(iota((32, 8, 16), 0), 2)
    fresh_col = iota((32, 8, 16), 2)
    fresh_ok = (lax.rem(fresh_col, 8) == iota((32, 8, 16), 1)) & (fresh_col // 8 <= lead)

    def attend(g):
        wide = pl.ds(pl.multiple_of(g * 2048, 2048), 2048)
        cols = pl.ds(pl.multiple_of(g * HD, HD), HD)
        flat = qbuf[:, wide]
        q = jnp.concatenate([flat[:, h * HD : (h + 1) * HD] for h in range(16)], axis=0)
        q_wide = jnp.concatenate([q * keep[r] for r in range(8)], axis=1)
        k_wide = jnp.concatenate([kbuf[r, :, cols] for r in range(8)], axis=1)
        scores = (nt_dot(q_wide, k_wide) * HD**-0.5).reshape(32, 8, CACHE)
        fresh = (nt_dot(q, new_keys[:, cols]) * HD**-0.5).reshape(32, 8, 16)
        peak = jnp.maximum(
            jnp.max(jnp.where(alive, scores, neg_fill), axis=2, keepdims=True),
            jnp.max(jnp.where(fresh_ok, fresh, neg_fill), axis=2, keepdims=True),
        )
        weights = jnp.where(alive, jnp.exp(scores - peak), 0.0)
        fresh_weights = jnp.where(fresh_ok, jnp.exp(jnp.minimum(fresh - peak, 0.0)), 0.0)
        total = jnp.sum(weights, axis=2, keepdims=True) + jnp.sum(
            fresh_weights, axis=2, keepdims=True
        )
        inverse = 1.0 / total
        probs = (weights * inverse).reshape(256, CACHE).astype(bf16)
        fresh_probs = (fresh_weights * inverse).reshape(256, 16).astype(bf16)
        p_wide = jnp.concatenate([probs * keep_wide[r] for r in range(8)], axis=1)
        v_tall = jnp.concatenate([vbuf[r, :, cols] for r in range(8)], axis=0)
        heads = nn_dot(p_wide, v_tall) + nn_dot(fresh_probs, new_values[:, cols])
        heads = heads.astype(bf16)
        for half in range(2):
            parts = [heads[(half * 8 + h) * 16 : (half * 8 + h + 1) * 16] for h in range(8)]
            sendh[2 * g + half] = jnp.concatenate(parts, axis=1)

    each(0, EARLY, attend)

    pl.semaphore_wait(barrier, MATES)

    swap = remote(mine, other, x0s.at[0], x0q.at[0], (partner, t))
    swap.start()
    swap.wait_recv()
    even = lax.rem(k, 2) == 0
    first = core == 0
    near_a = jnp.where(first, mine[:, :BLOCK], other[:, :BLOCK])
    near_b = jnp.where(first, other[:, :BLOCK], mine[:, :BLOCK])
    far_a = jnp.where(first, mine[:, BLOCK:], other[:, BLOCK:])
    far_b = jnp.where(first, other[:, BLOCK:], mine[:, BLOCK:])
    both[:, :BLOCK] = jnp.where(even, jnp.maximum(near_a, near_b), near_a)
    both[:, BLOCK:] = jnp.where(even, far_b, jnp.maximum(far_a, near_b))
    place_here = lax.rem(k, 2) * N_TP + t

    def x1(d):
        return remote(both, x1r.at[place_here], x1s.at[d], x1q.at[d], near_peer(d))

    unrolled(1, NEAR, lambda d: x1(d).start())
    x1r[place_here] = both[...]

    each(EARLY, KVH, attend)

    def send_heads(d):
        return remote(
            sendh.at[tp_peer(d)], recvh.at[t], hs.at[d], hq.at[d], (f, tp_peer(d))
        )

    unrolled(1, N_TP, lambda d: send_heads(d).start())
    recvh[t] = sendh[t]

    each(1, NEAR, lambda d: x1(d).wait_recv())
    quad = f // 4
    maxima = []
    for side in range(2):
        whole = x1r[side * N_TP]
        for j in range(1, N_TP):
            whole = jnp.maximum(whole, x1r[side * N_TP + j])
        maxima.append(whole)
    every[quad, 0] = maxima[0][:, :BLOCK]
    every[quad, 1] = jnp.maximum(maxima[0][:, BLOCK:], maxima[1][:, :BLOCK])
    every[quad, 2] = maxima[1][:, BLOCK:]

    def x2(d):
        to = 4 * lax.rem(quad + d, 4) + lax.rem(f, 4)
        return remote(every.at[quad], every.at[quad], x2s.at[d], x2q.at[d], (to, t))

    each(1, 4, lambda d: x2(d).start())

    near_tile = first_tile - 3 * quad
    scales = [
        (every[quad, near_tile] + epsilon) / fp_limit,
        (every[quad, jnp.minimum(near_tile + 1, 2)] + epsilon) / fp_limit,
    ]
    inverses = [tie_nudge / scale for scale in scales]

    def send_weights(m, d):
        return remote(
            sendw.at[m, d], wbuf.at[0, m, t], ws.at[m, d], wq.at[m, d], (f, tp_peer(d))
        )

    def convert_matrix(m):
        def restore(c, carry):
            here = lane == m * COLS + c
            near_scale, far_scale, near_inv, far_inv = (
                jnp.sum(jnp.where(here, table, 0.0), axis=1, keepdims=True)
                for table in scales + inverses
            )
            for i in range(SHARD):
                rows = slice(i * WIN, (i + 1) * WIN)
                value = mast[m, c, rows, :] * jnp.where(i < border, near_inv, far_inv)
                grid = value.astype(jnp.float8_e4m3fn).astype(f32)
                mast[m, c, rows, :] = grid * jnp.where(i < border, near_scale, far_scale)
            return carry

        lax.fori_loop(0, COLS, restore, 0, unroll=2)

        def convert(i):
            d = lax.rem(i, N_TP)
            e = tp_peer(d)

            def piece(c, carry):
                parts = [
                    mast[m, quarter * (QUARTER // BLOCK) + c, pl.ds(e, SHARD, stride=WIN), :]
                    for quarter in range(4)
                ]
                cols = pl.ds(pl.multiple_of(c * BLOCK, BLOCK), BLOCK)
                sendw[m, d, :, cols] = jnp.concatenate(parts, axis=0).astype(bf16)
                return carry

            lax.fori_loop(0, QUARTER // BLOCK, piece, 0, unroll=4)

            @pl.when(d != 0)
            def _():
                send_weights(m, d).start()

        each(1, N_TP + 1, convert)
        wbuf[0, m, t] = sendw[m, 0]

    convert_matrix(0)

    loads[4].wait()
    each(1, N_TP, lambda d: send_heads(d).wait_recv())

    def send_projected(s, d):
        return remote(
            sendp.at[s, d], recvp.at[s, t], ps.at[s, d], pq.at[s, d], (f, tp_peer(d))
        )

    def project(i):
        d = lax.rem(i, N_TP)
        cols = pl.ds(pl.multiple_of(tp_peer(d) * SHARE, SHARE), SHARE)
        rows = recvh[...].reshape(STEPS * ROWS, QH * HD // N_TP)
        result = nn_dot(rows, wproj[:, cols]).reshape(8, STEPS, 8, SHARE)
        for s in range(STEPS):
            sendp[s, d] = result[:, s].reshape(ROWS, SHARE).astype(bf16)

        @pl.when(d != 0)
        def _():
            send_projected(0, d).start()

    each(1, N_TP + 1, project)
    for s in range(STEPS):
        recvp[s, t] = sendp[s, 0]
    loads[3].wait()

    convert_matrix(1)
    convert_matrix(2)

    def pass_on(d):
        origin = lax.rem(t + N_TP - d, N_TP)
        return remote(
            wbuf.at[0, :, origin], wbuf.at[1, :, origin], cs.at[d], cq.at[d], (partner, t)
        )

    pass_on(0).start()

    quarter_of = lax.rem(iota((WIN * CAP, 8 * FOLD), 1), FOLD) // SHARD

    def send_slots(s, d):
        return remote(
            sendd.at[s, tp_peer(d)], recvd.at[s, t], ds.at[s, d], dq.at[s, d], (f, tp_peer(d))
        )

    def send_normed(s, d):
        to = 2 * chip_peer(d) + core
        return remote(sende.at[s], recve.at[s, k], es.at[s, d], eq.at[s, d], (to, t))

    def send_partial(s, d):
        to = chip_peer(d // N_TP) * N_TP + tp_peer(d % N_TP)
        return remote(
            sendg.at[s, pl.ds(pl.multiple_of(to * 16, 16), 16)],
            recvg.at[s, pl.ds(pl.multiple_of((k * N_TP + t) * 16, 16), 16)],
            gs.at[s],
            gq.at[s],
            mate(d),
        )

    def all_partials(s):
        most = slice(0, (MATES - 1) * 16)
        return remote(sendg.at[s, most], recvg.at[s, most], gs.at[s], gq.at[s], (partner, t))

    def gathered(s, half, m):
        rows = recve[s].reshape(128, 2048)
        rows = jnp.concatenate([rows[:, :QUARTER], rows[:, QUARTER:]], axis=0)
        product = nt_dot(rows, wbuf[half, m].reshape(8 * FOLD, QUARTER))
        product = product.reshape(2, 8, 2, CAP, 8 * FOLD)
        by = [product[q % 2, :, q // 2].reshape(WIN * CAP, 8 * FOLD) for q in range(4)]
        parts = jnp.where(
            quarter_of == 0,
            by[0],
            jnp.where(quarter_of == 1, by[1], jnp.where(quarter_of == 2, by[2], by[3])),
        )
        high = parts.astype(bf16)
        rest = parts - high.astype(f32)
        middle = rest.astype(bf16)
        low = (rest - middle.astype(f32)).astype(bf16)
        split = nn_dot(jnp.concatenate([high, middle, low], axis=0), spread[...])
        split = split.reshape(3, WIN * CAP, 8 * FOLD)
        return split[0] + split[1] + split[2]

    def drain_early(d):
        send_heads(d).wait_send()
        for m in range(3):
            send_weights(m, d).wait_send()
        send_projected(0, d).wait_send()

    def decode(s):
        each(1, N_TP, lambda d: send_projected(s, d).wait_recv())
        projected = recvp[s, 0].astype(f32)
        for j in range(1, N_TP):
            projected = projected + recvp[s, j].astype(f32)
        mix = (cur[...].astype(f32) + projected).astype(bf16)
        mixed[s] = mix
        sendd[s] = nn_dot(slots[s], mix).reshape(WIN, CAP, SHARE)
        unrolled(1, N_TP, lambda d: send_slots(s, d).start())
        recvd[s, t] = sendd[s, t]
        each(1, N_TP, lambda d: send_slots(s, d).wait_recv())
        blocks = [recvd[s, j] for j in range(N_TP)]
        squares = blocks[0] * blocks[0]
        for block in blocks[1:]:
            squares = squares + block * block
        squares = jnp.sum(squares, axis=1, keepdims=True)
        inverse = lax.rsqrt(squares * (1.0 / D) + epsilon)
        normed = [
            blocks[j] * inverse * gain[:, j * SHARE : (j + 1) * SHARE] for j in range(N_TP)
        ]
        folded = jnp.concatenate(
            [jnp.concatenate(normed[:4], axis=1), jnp.concatenate(normed[4:], axis=1)], axis=0
        ).astype(bf16)
        sende[s] = folded
        unrolled(1, 8, lambda d: send_normed(s, d).start())
        recve[s, k] = folded

        @pl.when(s == 0)
        def _():
            each(1, 4, lambda d: x2(d).wait_recv())
            for tile in range(TILES):
                log = jnp.log2((every[tile // 3, tile % 3] + epsilon) / fp_limit)
                for m in range(3):
                    logs[m, tile] = log[:, m * COLS : (m + 1) * COLS]

            def forward(d):
                for m in range(3):
                    send_weights(m, d).wait_recv()
                pass_on(d).start()

            each(1, N_TP, forward)
            each(1, N_TP, lambda d: send_projected(1, d).start())
            each(0, N_TP, lambda d: pass_on(d).wait_recv())

        each(1, 8, lambda d: send_normed(s, d).wait_recv())
        total = jnp.zeros((4 * WIN * CAP, QUARTER), f32)
        for half in range(2):
            gate = gathered(s, half, 0)
            up = gathered(s, half, 1)
            act = gate / (1.0 + jnp.exp(-gate)) * up
            stacked = jnp.concatenate(
                [jnp.where(quarter_of == q, act, 0.0) for q in range(4)], axis=0
            ).astype(bf16)
            total = total + nn_dot(stacked, wbuf[half, 2].reshape(8 * FOLD, QUARTER))
        total = total.reshape(4, 8, CAP, QUARTER)
        folds = []
        for j in range(N_TP):
            block = total[j // 2, :, :, (j % 2) * SHARE : (j % 2 + 1) * SHARE]
            folds.append(jnp.concatenate([block[..., : SHARE // 2], block[..., SHARE // 2 :]], axis=1))
        folds = jnp.stack(folds, axis=1).astype(bf16)
        sendg[s] = folds.reshape(MATES * 16, SHARE // 2)
        unrolled(1, MATES, lambda d: send_partial(s, d).start())
        here = pl.ds(pl.multiple_of((k * N_TP + t) * 16, 16), 16)
        recvg[s, here] = sendg[s, here]

        @pl.when(s == 0)
        def _():
            swap.wait_send()
            each(1, NEAR, lambda d: x1(d).wait_send())
            each(1, 4, lambda d: x2(d).wait_send())
            each(0, N_TP, lambda d: pass_on(d).wait_send())
            each(1, N_TP, drain_early)

        all_partials(s).wait_recv()
        block_rows = N_TP * 16
        summed = recvg[s, :block_rows].astype(f32)
        for j in range(1, 8):
            summed = summed + recvg[s, j * block_rows : (j + 1) * block_rows].astype(f32)
        summed = summed.reshape(WIN, 2, CAP, SHARE // 2)
        summed = jnp.concatenate([summed[:, 0], summed[:, 1]], axis=2).reshape(WIN * CAP, SHARE)
        returned = (summed * share[s, :, :1]).astype(bf16)
        moe = nn_dot(slots_t[s], returned)
        cur[...] = (mixed[s].astype(f32) + moe).astype(bf16)

    each(0, STEPS, decode)
    out[...] = cur[...]

    def drain(d):
        send_projected(1, d).wait_send()
        for s in range(STEPS):
            send_slots(s, d).wait_send()
            send_normed(s, d).wait_send()

    each(1, N_TP, drain)
    for s in range(STEPS):
        all_partials(s).wait_send()


def local(
    hidden_in,
    queries,
    key_cache,
    value_cache,
    new_keys,
    new_values,
    lengths,
    routes,
    route_weights,
    norm_gain,
    gate_master,
    up_master,
    down_master,
    out_proj,
):
    def flat(master):
        blocks = master.transpose(1, 0, 2).reshape(SHARD, WIN, COLS, BLOCK)
        return blocks.transpose(0, 2, 1, 3)

    vmem = pl.BlockSpec(memory_space=pltpu.VMEM)
    smem = pl.BlockSpec(memory_space=pltpu.SMEM)
    far = pl.BlockSpec(memory_space=pl.ANY)
    dma = pltpu.SemaphoreType.DMA
    v = pltpu.VMEM
    scratch = [
        v((3, COLS, SHARD * WIN, BLOCK), f32),
        v((16, QH * HD), bf16),
        v((8, CACHE, KVH * HD), bf16),
        v((8, CACHE, KVH * HD), bf16),
        v((QH * HD // N_TP, D), bf16),
        v((ROWS, SHARE), bf16),
        v((WIN, 2 * BLOCK), f32),
        v((WIN, 2 * BLOCK), f32),
        v((WIN, 2 * BLOCK), f32),
        v((NEAR, WIN, 2 * BLOCK), f32),
        v((4, 3, WIN, BLOCK), f32),
        v((3, N_TP, FOLD, QUARTER), bf16),
        v((2, 3, N_TP, FOLD, QUARTER), bf16),
        v((N_TP, 16, 1024), bf16),
        v((N_TP, 16, 1024), bf16),
        v((STEPS, N_TP, ROWS, SHARE), bf16),
        v((STEPS, N_TP, ROWS, SHARE), bf16),
        v((STEPS, WIN * CAP, ROWS), bf16),
        v((STEPS, ROWS, WIN * CAP), bf16),
        v((STEPS, WIN * CAP, BLOCK), f32),
        v((STEPS, ROWS, SHARE), bf16),
        v((STEPS, WIN, CAP, SHARE), f32),
        v((STEPS, N_TP, CAP, SHARE), f32),
        v((STEPS, 16, 2048), bf16),
        v((STEPS, 8, 16, 2048), bf16),
        v((STEPS, MATES * 16, SHARE // 2), bf16),
        v((STEPS, MATES * 16, SHARE // 2), bf16),
        v((8 * FOLD, 8 * FOLD), bf16),
        dma((8,)),
        dma((1,)),
        dma((1,)),
        dma((NEAR,)),
        dma((NEAR,)),
        dma((4,)),
        dma((4,)),
        dma((N_TP,)),
        dma((N_TP,)),
        dma((3, N_TP)),
        dma((3, N_TP)),
        dma((N_TP,)),
        dma((N_TP,)),
    ]
    scratch += [dma((STEPS, N_TP)) for _ in range(6)]
    scratch += [dma((STEPS,)) for _ in range(2)]
    out, logs = pl.pallas_call(
        kernel,
        out_shape=(
            jax.ShapeDtypeStruct((ROWS, SHARE), bf16),
            jax.ShapeDtypeStruct((3, TILES, WIN, COLS), f32),
        ),
        in_specs=[far, far, far, far, vmem, vmem, smem, vmem, vmem, vmem, far, far, far, far],
        out_specs=(vmem, vmem),
        scratch_shapes=scratch,
        compiler_params=pltpu.CompilerParams(
            collective_id=0, has_side_effects=True, vmem_limit_bytes=58 << 20
        ),
    )(
        hidden_in,
        queries.reshape(16, QH * HD),
        key_cache,
        value_cache,
        new_keys.reshape(16, KVH * HD),
        new_values.reshape(16, KVH * HD),
        lengths,
        routes.transpose(0, 2, 1),
        route_weights.transpose(0, 2, 1),
        norm_gain.reshape(1, D),
        flat(gate_master),
        flat(up_master),
        flat(down_master),
        out_proj,
    )
    return (out, logs.transpose(0, 2, 1, 3))


def solution(mesh):
    in_specs = (
        P("fsdp", None),
        P(None, ("fsdp", "tp"), None),
        P(("fsdp", "tp"), None, None),
        P(("fsdp", "tp"), None, None),
        P(None, ("fsdp", "tp"), None),
        P(None, ("fsdp", "tp"), None),
        P(("fsdp", "tp")),
        P(None, "fsdp", None),
        P(None, "fsdp", None),
        P(),
        P(None, ("fsdp", "tp"), None),
        P(None, ("fsdp", "tp"), None),
        P(None, ("fsdp", "tp"), None),
        P("tp", None),
    )
    out_specs = (P("fsdp", "tp"), P())
    return jax.shard_map(local, mesh=mesh, in_specs=in_specs, out_specs=out_specs, check_vma=False)
```
